32 devices in a mesh: row: 8 (over z, x), col: 4 (over y, core).
Axes of the slice: x: 2, y: 2, z: 4, core: 2. Of those that a mesh axis runs over, the one named last changes fastest.
Arguments:
- trailing: float32 [16, 4, 512, 512], P('row', 'col'), may hold values from -6 to 6
- panel_block: float32 [16, 512, 1024], P('row', 'col'), may hold values from -2.5 to 2.5
- diag_block: float32 [1024, 1024], P('row'), as said below
- tile_map: int32 [16], replicated, may hold values from 0 to 15, each once
Outputs:
- updated_trailing: float32 [16, 4, 512, 512], P('row', 'col')
- panel_factor: float32 [16, 512, 1024], P('row', 'col')
- diag_factor: float32 [1024, 1024], P('row')
The draws below stay inside these ranges and needn't reach their ends.
Inputs may be any that keep to these rules, and one draw needn't show every extreme that they name: `tile_map`: each of the 16 trailing tile rows stands in exactly one slot. `diag_block`: symmetric and positive definite.
All inputs are finite; a program needn't handle non-finite values.
Results may differ from the reference program's by a relative error of at most 0.0003.
Values sent between devices are 32-bit elements; how exact they have to be, the bound alone decides.
No kernel may reach another device: no remote copies, remote signals or barrier semaphores. Data moves between devices by JAX's collectives and lax.ppermute only.
A program may use at most 128 MiB of HBM per device.

```python
import jax
import jax.numpy as jnp
from jax import lax

TILE = 512
PW = 1024
NT = 16
N_COL = 4


def draw_diag_block(key, part):
    key_values, key_diag = jax.random.split(jax.random.fold_in(key, 7), 2)
    uniform_draw = jax.random.uniform(key_values, (PW, PW), jnp.float32, -1.0, 1.0)
    spread = 0.25 * 1.5 ** 0.5 / PW ** 0.5
    symmetric = (uniform_draw + uniform_draw.T) * spread
    identity = jnp.eye(PW, dtype=jnp.float32)
    diag_lift = jax.random.uniform(key_diag, (PW,), jnp.float32, 1.0, 2.0)
    matrix = symmetric * (1.0 - identity) + identity * diag_lift[None, :]
    return matrix


def levels(rng, shape, pieces, smallest, high):
    level = 1.0
    for position, blocks in pieces:
        steps = jax.random.uniform(jax.random.fold_in(jax.random.fold_in(rng, 6), position), (blocks,), jnp.float32, smallest / len(pieces), high / len(pieces))
        level = level * jnp.repeat(jnp.exp(steps), shape[position] // blocks).reshape((-1,) + (1,) * (len(shape) - 1 - position))
    return level


def bell_draw(rng, dims, deviation, most, pieces=(), held_as=jnp.bfloat16):
    drawn = jax.random.normal(rng, dims, jnp.float32) * deviation
    if len(pieces) > 0:
        drawn = levels(rng, dims, pieces, -0.22, 0.18) * drawn
    return jnp.clip(drawn, min=-most, max=most).astype(held_as)


def setup_inputs(seed: int = 0) -> dict:
    streams_of = jax.random.split(jax.random.key(seed), 5)
    return {
        "trailing": bell_draw(streams_of[0], (NT, N_COL, TILE, TILE), 1.0, 6.0, ((0, 8), (1, 4)), jnp.float32),
        "panel_block": bell_draw(streams_of[1], (NT, TILE, PW), 0.18, 2.5, ((0, 8), (1, 4)), jnp.float32),
        "diag_block": draw_diag_block(jax.random.fold_in(streams_of[4], 71), 0),
        "tile_map": jax.random.permutation(streams_of[3], NT).astype(jnp.int32),
    }


def solve_rows(factor, row_block):
    flattened = row_block.reshape(-1, row_block.shape[-1])
    solved = lax.linalg.triangular_solve(factor, flattened, left_side=False, lower=True, transpose_a=True)
    return solved.reshape(row_block.shape)

def reference(trailing, panel_block, diag_block, tile_map):
    diag_factor = jnp.linalg.cholesky(diag_block)
    panel_factor = solve_rows(diag_factor, panel_block)
    slot_index = jnp.arange(tile_map.shape[0], dtype=jnp.int32)
    column_ids = jnp.arange(N_COL, dtype=jnp.int32)
    owner_slot = jnp.sum(jnp.where(tile_map[None, :] == column_ids[:, None], slot_index[None, :], 0), axis=1).astype(jnp.int32)
    column_panel = panel_factor[owner_slot]

    def update(slot_data):
        tile_rows, slot_panel, tile_id = slot_data
        products = jnp.einsum('ak,cbk->cab', slot_panel, column_panel, precision=lax.Precision.HIGHEST)
        tile_live = tile_id >= column_ids
        return jnp.where(tile_live[:, None, None], tile_rows - products, jnp.zeros_like(tile_rows))
    updated_trailing = lax.map(update, (trailing, panel_factor, tile_map))
    return (updated_trailing, panel_factor, diag_factor)
```

```python
import functools

import jax
import jax.numpy as jnp
from jax import lax
from jax.experimental import pallas as pl
from jax.experimental.pallas import tpu as pltpu
from jax.sharding import PartitionSpec as P

BLOCK = 128
WIDE = 256
F32, BF16 = jnp.float32, jnp.bfloat16


def spread_row(x, m):
    return jnp.broadcast_to(x[m : m + 1, :], x.shape)


def spread_lane(x, j):
    return jnp.broadcast_to(x[:, j : j + 1], x.shape)


def inverse_of(d):
    guess = pl.reciprocal(d, approx=True)
    return guess * (2.0 - d * guess)


def factor_block(rows_in):
    count = len(rows_in)
    work = list(rows_in)
    lane = lax.broadcasted_iota(jnp.int32, (8, BLOCK), 1)
    sub = lax.broadcasted_iota(jnp.int32, (8, BLOCK), 0)
    upper, inverse = [], []
    for b in range(count):
        o = 8 * b
        rows = [spread_row(work[b], m) for m in range(8)]
        p = {(m, l): spread_lane(rows[m], o + l) for m in range(8) for l in range(m + 1)}
        r = list(rows)
        t = [jnp.where(lane == o + m, 1.0, jnp.where(lane >= o, 0.0, rows[m])) for m in range(8)]
        f, ri = {}, []
        for j in range(8):
            ri.append(inverse_of(p[j, j]))
            for m in range(j + 1, 8):
                f[m, j] = p[m, j] * ri[j]
                for l in range(j + 1, m + 1):
                    p[m, l] = p[m, l] - f[m, j] * p[l, j]
                r[m] = r[m] - f[m, j] * r[j]
                t[m] = t[m] - f[m, j] * t[j]
        up, inv = None, None
        for m in range(8):
            s = lax.rsqrt(p[m, m])
            um, im = r[m] * s, t[m] * s
            up = um if m == 0 else jnp.where(sub == m, um, up)
            inv = im if m == 0 else jnp.where(sub == m, im, inv)
        upper.append(jnp.where(lane >= sub + o, up, 0.0))
        inverse.append(inv)
        if b + 1 < count:
            z = [None] * 8
            for m in range(7, -1, -1):
                v = jnp.where(lane < o + 8, t[m], r[m]) * ri[m]
                for l in range(7, m, -1):
                    v = v - f[l, m] * z[l]
                z[m] = v
            for i in range(b + 1, count):
                v = jnp.where((lane >= o) & (lane < o + 8), 0.0, work[i])
                for m in range(8):
                    v = v - spread_lane(work[i], o + m) * z[m]
                work[i] = v
    return upper, inverse


def dot_nt(a, b, precision=None):
    return lax.dot_general(a, b, (((1,), (1,)), ((), ())), precision=precision, preferred_element_type=F32)


def full_nt(a, b):
    return dot_nt(a, b, lax.Precision.HIGHEST)


def halves(x):
    high = x.astype(BF16)
    return high, (x - high.astype(F32)).astype(BF16)


def split_nt(ah, al, bh, bl):
    return dot_nt(ah, bh) + (dot_nt(ah, bl) + dot_nt(al, bh))


def cholesky_kernel(n_row, where_ref, *refs):
    pieces = refs[: 2 * n_row]
    own_ref, lh_ref, ll_ref, wh_ref, wl_ref, a_ref, l_ref, w_ref, s_ref, t_ref, sem = refs[2 * n_row :]
    n = a_ref.shape[0]
    count = n // BLOCK
    rows = n // n_row
    width = n // 2
    row, core = where_ref[0], where_ref[2]
    copies = []
    for i, piece in enumerate(pieces):
        source, side = row ^ (i // 2), core ^ (i % 2)
        target = a_ref.at[
            pl.ds(pl.multiple_of(source * rows, rows), rows), pl.ds(pl.multiple_of(side * width, width), width)
        ]
        copies.append(pltpu.make_async_copy(piece, target, sem.at[i]))
    for copy in copies:
        copy.start()
    for copy in copies:
        copy.wait()
    s_ref[...] = a_ref[:, 0:BLOCK]

    @pl.loop(0, count)
    def _(k):
        upper, inverse = factor_block([s_ref[8 * i : 8 * i + 8, :] for i in range(BLOCK // 8)])
        for i in range(BLOCK // 8):
            t_ref[8 * i : 8 * i + 8, :] = upper[i]
            w_ref[k, 8 * i : 8 * i + 8, :] = inverse[i]
        for step in range(count):

            @pl.when(k == step)
            def _():
                lo, hi = step * BLOCK, step * BLOCK + BLOCK
                left = n - hi
                l_ref[lo:hi, lo:hi] = t_ref[...].T
                if left:
                    l_ref[lo:hi, hi:] = jnp.zeros((BLOCK, left), F32)
                    l_ref[hi:, lo:hi] = full_nt(s_ref[BLOCK : BLOCK + left, :], w_ref[step])
                    s_ref[0:left, :] = a_ref[hi:, hi : hi + BLOCK] - full_nt(l_ref[hi:, :hi], l_ref[hi : hi + BLOCK, :hi])

    own_ref[...] = l_ref[pl.ds(pl.multiple_of(row * rows, rows), rows), :]
    lh_ref[...], ll_ref[...] = halves(l_ref[...])
    for k in range(n // WIDE):
        lo = k * WIDE
        first, second = w_ref[2 * k], w_ref[2 * k + 1]
        cross = l_ref[lo + BLOCK : lo + WIDE, lo : lo + BLOCK]
        mixed = jnp.dot(cross, first, precision=lax.Precision.HIGHEST, preferred_element_type=F32)
        corner = -jnp.dot(second, mixed, precision=lax.Precision.HIGHEST, preferred_element_type=F32)
        whole = jnp.concatenate(
            [jnp.concatenate([first, jnp.zeros_like(first)], 1), jnp.concatenate([corner, second], 1)], 0
        )
        wh_ref[k], wl_ref[k] = halves(whole)


def cholesky(where, pieces, n, n_row):
    count = n // BLOCK
    vmem, smem = pl.BlockSpec(memory_space=pltpu.VMEM), pl.BlockSpec(memory_space=pltpu.SMEM)
    return pl.pallas_call(
        functools.partial(cholesky_kernel, n_row),
        out_shape=(
            jax.ShapeDtypeStruct((n // n_row, n), F32),
            jax.ShapeDtypeStruct((n, n), BF16),
            jax.ShapeDtypeStruct((n, n), BF16),
            jax.ShapeDtypeStruct((n // WIDE, WIDE, WIDE), BF16),
            jax.ShapeDtypeStruct((n // WIDE, WIDE, WIDE), BF16),
        ),
        in_specs=[smem] + [pl.BlockSpec(memory_space=pl.ANY)] * len(pieces),
        out_specs=[vmem] * 5,
        scratch_shapes=[
            pltpu.VMEM((n, n), F32),
            pltpu.VMEM((n, n), F32),
            pltpu.VMEM((count, BLOCK, BLOCK), F32),
            pltpu.VMEM((n, BLOCK), F32),
            pltpu.VMEM((BLOCK, BLOCK), F32),
            pltpu.SemaphoreType.DMA((len(pieces),)),
        ],
        compiler_params=pltpu.CompilerParams(vmem_limit_bytes=40 * 2**20),
        cost_estimate=pl.CostEstimate(flops=8 * n**3, bytes_accessed=12 * n * n, transcendentals=0),
        name="cholesky",
    )(where, *pieces)


def solve(source, xh_ref, xl_ref, lh_ref, ll_ref, wh_ref, wl_ref, keep=None):
    n = lh_ref.shape[0]
    for k in range(n // WIDE):
        lo, hi = k * WIDE, k * WIDE + WIDE
        rest = source[:, lo:hi]
        if k:
            rest = rest - split_nt(xh_ref[:, :lo], xl_ref[:, :lo], lh_ref[lo:hi, :lo], ll_ref[lo:hi, :lo])
        rh, rl = halves(rest)
        x = split_nt(rh, rl, wh_ref[k], wl_ref[k])
        if keep is not None:
            keep(lo, hi, x)
        xh_ref[:, lo:hi], xl_ref[:, lo:hi] = halves(x)


def rows_kernel(*refs):
    n_piece = len(refs) - 9
    pieces = refs[:n_piece]
    lh_ref, ll_ref, wh_ref, wl_ref, own_ref, xh_ref, xl_ref, p_ref, sem = refs[n_piece:]
    slots, rows, n = pieces[0].shape
    copies = [pltpu.make_async_copy(piece, p_ref.at[i], sem.at[i]) for i, piece in enumerate(pieces)]
    for copy in copies:
        copy.start()

    @pl.loop(0, n_piece)
    def _(i):
        pltpu.make_async_copy(pieces[0], p_ref.at[i], sem.at[i]).wait()

        def keep(lo, hi, x):
            @pl.when(i == 0)
            def _():
                own_ref[:, :, lo:hi] = x.reshape(slots, rows, hi - lo)

        source = p_ref.at[i].reshape(slots * rows, n)
        solve(source, xh_ref.at[i], xl_ref.at[i], lh_ref, ll_ref, wh_ref, wl_ref, keep)


def factor_rows(pieces, factor):
    slots, rows, n = pieces[0].shape
    vmem = pl.BlockSpec(memory_space=pltpu.VMEM)
    count = len(pieces)
    return pl.pallas_call(
        rows_kernel,
        out_shape=(
            jax.ShapeDtypeStruct((slots, rows, n), F32),
            jax.ShapeDtypeStruct((count, slots * rows, n), BF16),
            jax.ShapeDtypeStruct((count, slots * rows, n), BF16),
        ),
        in_specs=[pl.BlockSpec(memory_space=pl.ANY)] * count + [vmem] * 4,
        out_specs=[vmem] * 3,
        scratch_shapes=[pltpu.VMEM((count, slots, rows, n), F32), pltpu.SemaphoreType.DMA((count,))],
        compiler_params=pltpu.CompilerParams(vmem_limit_bytes=40 * 2**20),
        cost_estimate=pl.CostEstimate(flops=6 * count * slots * rows * n * n, bytes_accessed=20 * n * n, transcendentals=0),
        name="factor_rows",
    )(*pieces, *factor)


def update_kernel(n_piece, where_ref, p_ref, lh_ref, ll_ref, wh_ref, wl_ref, xh_ref, xl_ref, t_ref, out_ref, ch_ref, cl_ref):
    slots, _, tile, _ = t_ref.shape
    rows = tile // n_piece
    col = where_ref[1]
    solve(p_ref, ch_ref, cl_ref, lh_ref, ll_ref, wh_ref, wl_ref)

    @pl.loop(0, n_piece)
    def _(i):
        at = pl.ds(pl.multiple_of((col ^ i) * rows, rows), rows)
        product = split_nt(xh_ref[i], xl_ref[i], ch_ref[...], cl_ref[...])
        for s in range(slots):
            live = where_ref[3 + s] > 0
            new = t_ref[s, 0, at, :] - product[s * rows : (s + 1) * rows]
            out_ref[s, 0, at, :] = jnp.where(live, new, jnp.zeros_like(new))


def update(where, column, factor, xh, xl, trailing):
    tile, n = column.shape
    vmem, smem = pl.BlockSpec(memory_space=pltpu.VMEM), pl.BlockSpec(memory_space=pltpu.SMEM)
    return pl.pallas_call(
        functools.partial(update_kernel, xh.shape[0]),
        out_shape=jax.ShapeDtypeStruct(trailing.shape, F32),
        in_specs=[smem] + [vmem] * 8,
        out_specs=vmem,
        scratch_shapes=[pltpu.VMEM((tile, n), BF16), pltpu.VMEM((tile, n), BF16)],
        compiler_params=pltpu.CompilerParams(vmem_limit_bytes=40 * 2**20),
        cost_estimate=pl.CostEstimate(flops=10 * tile * n * n, bytes_accessed=20 * n * n, transcendentals=0),
        name="update",
    )(where, column, *factor, xh, xl, trailing)


def flip(x, axis, size, bit):
    return lax.ppermute(x, axis, [(i, i ^ bit) for i in range(size)])


def gather_flips(x, axis, size):
    found = {0: x}
    bit = size // 2
    while bit:
        for p in list(found):
            found[p | bit] = flip(found[p], axis, size, bit)
        bit //= 2
    return [found[p] for p in range(size)]


def per_device(n_row, n_col, trailing, panel_block, diag_block, tile_map):
    slots, rows, n = panel_block.shape
    tile = rows * n_col
    row, col = lax.axis_index("row"), lax.axis_index("col")
    slot_index = jnp.arange(tile_map.shape[0], dtype=jnp.int32)
    own_tiles = lax.dynamic_slice_in_dim(tile_map, row * slots, slots)
    live = (own_tiles >= col).astype(jnp.int32)
    where = jnp.concatenate([jnp.stack([row, col, col & 1]).astype(jnp.int32), live])

    side = lax.dynamic_slice_in_dim(diag_block, (col & 1) * (n // 2), n // 2, 1)
    other = lax.dynamic_slice_in_dim(diag_block, (1 - (col & 1)) * (n // 2), n // 2, 1)
    mine = gather_flips(side, "row", n_row)
    theirs = [other] + [flip(x, "col", n_col, 1) for x in mine[1:]]
    diag_pieces = [x for pair in zip(mine, theirs) for x in pair]

    row_pieces = gather_flips(panel_block, "col", n_col)

    chunk = rows // n_row
    parts = panel_block.reshape(slots, n_row, chunk, n).transpose(1, 0, 2, 3)
    parts = lax.all_to_all(parts, "row", 0, 0, tiled=True).reshape(n_row * slots, chunk, n)
    chosen = []
    for c in range(n_col):
        slot = jnp.sum(jnp.where(tile_map == c, slot_index, 0))
        chosen.append(lax.dynamic_index_in_dim(parts, slot, 0, keepdims=False))
    own_column = lax.all_to_all(jnp.stack(chosen), "col", 0, 0, tiled=True)
    chunks = jnp.stack(gather_flips(own_column, "row", n_row))
    order = jnp.arange(n_row, dtype=jnp.int32) ^ row
    column = chunks[order].transpose(1, 0, 2, 3).reshape(tile, n)

    diag_factor, *factor = cholesky(where, diag_pieces, n, n_row)
    panel_factor, xh, xl = factor_rows(row_pieces, factor)
    updated = update(where, column, factor, xh, xl, trailing)
    return updated, panel_factor, diag_factor


def solution(mesh):
    n_row, n_col = mesh.shape["row"], mesh.shape["col"]
    in_specs = (P("row", "col", None, None), P("row", "col", None), P("row", None), P())
    out_specs = (P("row", "col", None, None), P("row", "col", None), P("row", None))
    return jax.shard_map(
        functools.partial(per_device, n_row, n_col),
        mesh=mesh,
        in_specs=in_specs,
        out_specs=out_specs,
        check_vma=False,
    )
```

```python
import functools

import jax
import jax.numpy as jnp
from jax import lax
from jax.experimental import pallas as pl
from jax.experimental.pallas import tpu as pltpu
from jax.sharding import PartitionSpec as P

BLOCK = 128
WIDE = 256
F32, BF16 = jnp.float32, jnp.bfloat16


def spread_row(x, m):
    return jnp.broadcast_to(x[m : m + 1, :], x.shape)


def spread_lane(x, j):
    return jnp.broadcast_to(x[:, j : j + 1], x.shape)


def factor_block(rows_in):
    count = len(rows_in)
    work = list(rows_in)
    lane = lax.broadcasted_iota(jnp.int32, (8, BLOCK), 1)
    sub = lax.broadcasted_iota(jnp.int32, (8, BLOCK), 0)
    upper, inverse = [], []
    for b in range(count):
        o = 8 * b
        rows = [spread_row(work[b], m) for m in range(8)]
        p = {(m, l): spread_lane(rows[m], o + l) for m in range(8) for l in range(m + 1)}
        r = list(rows)
        t = [jnp.where(lane == o + m, 1.0, jnp.where(lane >= o, 0.0, rows[m])) for m in range(8)]
        inside = (lane >= o) & (lane < o + 8)
        following = None
        if b + 1 < count:
            c = [spread_lane(work[b + 1], o + m) for m in range(8)]
            following = jnp.where(inside, 0.0, work[b + 1])
        f, ri = {}, []
        for j in range(8):
            ri.append(pl.reciprocal(p[j, j], approx=True))
            for m in range(j + 1, 8):
                f[m, j] = p[m, j] * ri[j]
                for l in range(j + 1, m + 1):
                    p[m, l] = p[m, l] - f[m, j] * p[l, j]
                r[m] = r[m] - f[m, j] * r[j]
                t[m] = t[m] - f[m, j] * t[j]
            if following is not None:
                following = following - c[j] * (jnp.where(lane < o + 8, t[j], r[j]) * ri[j])
                for m in range(j + 1, 8):
                    c[m] = c[m] - c[j] * f[m, j]
        up, inv = None, None
        for m in range(8):
            s = lax.rsqrt(p[m, m])
            um, im = r[m] * s, t[m] * s
            up = um if m == 0 else jnp.where(sub == m, um, up)
            inv = im if m == 0 else jnp.where(sub == m, im, inv)
        upper.append(jnp.where(lane >= sub + o, up, 0.0))
        inverse.append(inv)
        if following is not None:
            work[b + 1] = following
        if b + 2 < count:
            z = [None] * 8
            for m in range(7, -1, -1):
                v = jnp.where(lane < o + 8, t[m], r[m]) * ri[m]
                for l in range(7, m, -1):
                    v = v - f[l, m] * z[l]
                z[m] = v
            for i in range(b + 2, count):
                v = jnp.where(inside, 0.0, work[i])
                for m in range(8):
                    v = v - spread_lane(work[i], o + m) * z[m]
                work[i] = v
    return upper, inverse


def dot_nt(a, b, precision=None):
    return lax.dot_general(a, b, (((1,), (1,)), ((), ())), precision=precision, preferred_element_type=F32)


def full_nt(a, b):
    return dot_nt(a, b, lax.Precision.HIGHEST)


def halves(x):
    high = x.astype(BF16)
    return high, (x - high.astype(F32)).astype(BF16)


def split_nt(ah, al, bh, bl):
    return dot_nt(ah, bh) + (dot_nt(ah, bl) + dot_nt(al, bh))


def flipped_place(index, count):
    place, bit = 0, 1
    while bit < count:
        place = place * 2 + (index & 1)
        index = index >> 1
        bit *= 2
    return place


def packed(n, n_row):
    return n_row * BLOCK == n


def own_vmem():
    return pl.BlockSpec(memory_space=pltpu.VMEM)


def pair_kernel(pair, n, n_row, where_ref, *refs):
    chunk = refs[:2]
    if pair:
        s_in, l_in = refs[2:4]
    l_out, wh_ref, wl_ref = refs[2 + 2 * (pair > 0) :][:3]
    s_out = refs[-5] if pair * WIDE + WIDE < n else None
    l_ref, s_ref, load_sem, store_sem = refs[-4:]
    row, core = where_ref[0], where_ref[2]
    half = chunk[0].shape[1]

    def rows_of(g, lo):
        at = flipped_place(row ^ g, n_row)
        a, b = chunk[0][at, :, lo : lo + BLOCK], chunk[1][at, :, lo : lo + BLOCK]
        return [jnp.where(core == 0, a, b), jnp.where(core == 0, b, a)]

    def column(k):
        if not packed(n, n_row):
            out = [rows_of(g, k * BLOCK) for g in range(k * BLOCK // (2 * half), n_row)]
            return jnp.concatenate(sum(out, []), 0)
        out = []
        for i in range(k, n_row):
            if 0 < i - k < n_row // 2:
                out.append(jnp.concatenate(rows_of(k, (i - k) * BLOCK), 0).T)
            else:
                out.append(jnp.concatenate(rows_of(i, (k - i) % n_row * BLOCK), 0))
        return jnp.concatenate(out, 0)

    begin = pair * WIDE
    loads = []
    if pair:
        region = (pl.ds(begin, n - begin), pl.ds(0, begin))
        loads.append(pltpu.make_async_copy(l_in.at[region], l_ref.at[region], load_sem))
        loads[0].start()
    else:
        s_ref[0] = column(0)
    stores, inverses = [], []
    for i in range(2):
        step = 2 * pair + i
        lo, hi = step * BLOCK, step * BLOCK + BLOCK
        source = s_in if pair and not i else s_ref.at[i]
        upper, inverse = factor_block([source[lo + 8 * j : lo + 8 * j + 8, :] for j in range(BLOCK // 8)])
        inverse = jnp.concatenate(inverse, 0)
        inverses.append(inverse)
        l_ref[lo:hi, lo:hi] = jnp.concatenate(upper, 0).T
        if hi < n:
            l_ref[hi:, lo:hi] = full_nt(source[hi:, :], inverse)
        region = (pl.ds(lo, n - lo), pl.ds(lo, BLOCK))
        stores.append(pltpu.make_async_copy(l_ref.at[region], l_out.at[region], store_sem.at[i]))
        stores[-1].start()
        if hi < n:
            if pair and not i:
                loads[0].wait()
            target = s_out if i else s_ref.at[1]
            target[hi:, :] = column(step + 1) - full_nt(l_ref[hi:, :hi], l_ref[hi : hi + BLOCK, :hi])
    first, second = inverses
    cross = l_ref[begin + BLOCK : begin + WIDE, begin : begin + BLOCK]
    mixed = jnp.dot(cross, first, precision=lax.Precision.HIGHEST, preferred_element_type=F32)
    corner = -jnp.dot(second, mixed, precision=lax.Precision.HIGHEST, preferred_element_type=F32)
    whole = jnp.concatenate(
        [jnp.concatenate([first, jnp.zeros_like(first)], 1), jnp.concatenate([corner, second], 1)], 0
    )
    wh_ref[...], wl_ref[...] = halves(whole)
    for copy in stores:
        copy.wait()


def cholesky_pair(pair, n, n_row, where, chunk, state):
    anywhere = pl.BlockSpec(memory_space=pl.ANY)
    last = pair * WIDE + WIDE == n
    square = jax.ShapeDtypeStruct((WIDE, WIDE), BF16)
    shapes = [jax.ShapeDtypeStruct((n, n), F32), square, square]
    if not last:
        shapes.append(jax.ShapeDtypeStruct((n, BLOCK), F32))
    l, wh, wl, *s = pl.pallas_call(
        functools.partial(pair_kernel, pair, n, n_row),
        out_shape=shapes,
        in_specs=[pl.BlockSpec(memory_space=pltpu.SMEM)] + [own_vmem()] * 2 + ([own_vmem(), anywhere] if pair else []),
        out_specs=[anywhere] + [own_vmem()] * (len(shapes) - 1),
        input_output_aliases={4: 0} if pair else {},
        scratch_shapes=[
            pltpu.VMEM((n, n), F32),
            pltpu.VMEM((2, n, BLOCK), F32),
            pltpu.SemaphoreType.DMA(()),
            pltpu.SemaphoreType.DMA((2,)),
        ],
        compiler_params=pltpu.CompilerParams(vmem_limit_bytes=16 * 2**20),
        cost_estimate=pl.CostEstimate(flops=14_000_000_000, bytes_accessed=4 * n * BLOCK * 4, transcendentals=0),
        name=f"cholesky_{pair}",
    )(where, *chunk, *state)
    return s + [l], wh, wl


def solve(source, xh_ref, xl_ref, lh_ref, ll_ref, wh_ref, wl_ref, keep_ref=None):
    n = lh_ref.shape[0]
    for k in range(n // WIDE):
        lo, hi = k * WIDE, k * WIDE + WIDE
        rest = source[:, lo:hi]
        if k:
            rest = rest - split_nt(xh_ref[:, :lo], xl_ref[:, :lo], lh_ref[lo:hi, :lo], ll_ref[lo:hi, :lo])
        rh, rl = halves(rest)
        x = split_nt(rh, rl, wh_ref[k][...], wl_ref[k][...])
        if keep_ref is not None:
            keep_ref[:, lo:hi] = x
        xh_ref[:, lo:hi], xl_ref[:, lo:hi] = halves(x)


def rows_kernel(n_row, n_piece, where_ref, *refs):
    pieces, l_in = refs[:n_piece], refs[n_piece]
    slots, rows, n = pieces[0].shape
    count, wide = n // BLOCK, n // WIDE
    refs = refs[n_piece + 1 :]
    wh_ref, wl_ref = refs[:wide], refs[wide : 2 * wide]
    own_ref, diag_ref, lh_ref, ll_ref, xh_ref, xl_ref, l_ref, p_ref, l_sem, p_sem = refs[2 * wide :]
    row, col = where_ref[0], where_ref[1]
    many = slots * rows
    l_copies, p_copies = [], []
    for k in range(count):
        region = (pl.ds(k * BLOCK, n - k * BLOCK), pl.ds(k * BLOCK, BLOCK))
        l_copies.append(pltpu.make_async_copy(l_in.at[region], l_ref.at[region], l_sem.at[k]))
    for i in range(n_piece):
        for t in range(slots):
            at = pl.multiple_of((col ^ i) * many + t * rows, rows)
            p_copies.append(
                pltpu.make_async_copy(pieces[i].at[t], p_ref.at[pl.ds(at, rows), :], p_sem.at[i * slots + t])
            )
    for copy in l_copies + p_copies:
        copy.start()
    for k, copy in enumerate(l_copies):
        copy.wait()
        lo, hi = k * BLOCK, k * BLOCK + BLOCK
        lh_ref[lo:, lo:hi], ll_ref[lo:, lo:hi] = halves(l_ref[lo:, lo:hi])
    share = n // n_row
    mine = l_ref[pl.ds(pl.multiple_of(row * share, share), share), :]
    block = lax.broadcasted_iota(jnp.int32, mine.shape, 1) // BLOCK
    diag_ref[...] = jnp.where(block <= row * share // BLOCK, mine, jnp.zeros_like(mine))
    for copy in p_copies:
        copy.wait()
    batch = 512

    @pl.loop(0, n_piece * many // batch)
    def _(i):
        at = pl.ds(pl.multiple_of(i * batch, batch), batch)
        solve(p_ref.at[at, :], xh_ref.at[at, :], xl_ref.at[at, :], lh_ref, ll_ref, wh_ref, wl_ref, p_ref.at[at, :])

    own_ref[...] = p_ref[pl.ds(pl.multiple_of(col * many, many), many), :].reshape(slots, rows, n)


def factor_rows(where, pieces, l, wh, wl, n_row):
    count = len(pieces)
    slots, rows, n = pieces[0].shape
    total = count * slots * rows
    anywhere = pl.BlockSpec(memory_space=pl.ANY)
    return pl.pallas_call(
        functools.partial(rows_kernel, n_row, count),
        out_shape=(
            jax.ShapeDtypeStruct((slots, rows, n), F32),
            jax.ShapeDtypeStruct((n // n_row, n), F32),
            jax.ShapeDtypeStruct((n, n), BF16),
            jax.ShapeDtypeStruct((n, n), BF16),
            jax.ShapeDtypeStruct((total, n), BF16),
            jax.ShapeDtypeStruct((total, n), BF16),
        ),
        in_specs=[pl.BlockSpec(memory_space=pltpu.SMEM)] + [anywhere] * (count + 1) + [own_vmem()] * (len(wh) + len(wl)),
        out_specs=[own_vmem()] * 6,
        scratch_shapes=[
            pltpu.VMEM((n, n), F32),
            pltpu.VMEM((total, n), F32),
            pltpu.SemaphoreType.DMA((n // BLOCK,)),
            pltpu.SemaphoreType.DMA((count * slots,)),
        ],
        compiler_params=pltpu.CompilerParams(vmem_limit_bytes=20 * 2**20),
        cost_estimate=pl.CostEstimate(flops=10_000_000_000, bytes_accessed=20 * n * n, transcendentals=0),
        name="factor_rows",
    )(where, *pieces, l, *wh, *wl)


def update_kernel(n_piece, places, where_ref, g_ref, lh_ref, ll_ref, xh_ref, xl_ref, t_ref, *refs):
    wide = g_ref.shape[2] // WIDE
    wh_ref, wl_ref = refs[:wide], refs[wide : 2 * wide]
    out_ref, p_ref, ch_ref, cl_ref = refs[2 * wide :]
    slots, _, tile, _ = t_ref.shape
    rows = tile // n_piece
    row = where_ref[0]
    chunk = g_ref.shape[1]
    for i, at in enumerate(places(row)):
        p_ref[i * chunk : i * chunk + chunk, :] = g_ref[at]
    solve(p_ref, ch_ref, cl_ref, lh_ref, ll_ref, wh_ref, wl_ref)

    @pl.loop(0, n_piece)
    def _(i):
        at = pl.ds(pl.multiple_of(i * rows, rows), rows)
        many = pl.ds(pl.multiple_of(i * (slots * rows), slots * rows), slots * rows)
        product = split_nt(xh_ref[many, :], xl_ref[many, :], ch_ref[...], cl_ref[...])
        for s in range(slots):
            live = where_ref[3 + s] > 0
            new = t_ref[s, 0, at, :] - product[s * rows : (s + 1) * rows]
            out_ref[s, 0, at, :] = jnp.where(live, new, jnp.zeros_like(new))


def update(where, n_piece, gathered, places, lh, ll, wh, wl, xh, xl, trailing):
    tile = trailing.shape[2]
    n = gathered.shape[2]
    return pl.pallas_call(
        functools.partial(update_kernel, n_piece, places),
        out_shape=jax.ShapeDtypeStruct(trailing.shape, F32),
        in_specs=[pl.BlockSpec(memory_space=pltpu.SMEM)] + [own_vmem()] * (6 + len(wh) + len(wl)),
        out_specs=own_vmem(),
        scratch_shapes=[pltpu.VMEM((tile, n), F32), pltpu.VMEM((tile, n), BF16), pltpu.VMEM((tile, n), BF16)],
        compiler_params=pltpu.CompilerParams(vmem_limit_bytes=20 * 2**20),
        cost_estimate=pl.CostEstimate(flops=10_000_000_000, bytes_accessed=20 * n * n, transcendentals=0),
        name="update",
    )(where, gathered, lh, ll, xh, xl, trailing, *wh, *wl)


def flip(x, axis, size, bit):
    return lax.ppermute(x, axis, [(i, i ^ bit) for i in range(size)])


def grow(x, axis, size, bit):
    return jnp.concatenate([x, flip(x, axis, size, bit)], 0)


def bits_of(size):
    return [size >> i for i in range(1, size.bit_length())]


def swap(x, axis, size):
    me = lax.axis_index(axis)
    found = x.reshape((size, 1) + x.shape[1:])
    bit = size // 2
    while bit:
        width = found.shape[0] // 2
        upper = (me & bit) > 0
        low, high = found[:width], found[width:]
        got = flip(jnp.where(upper, low, high), axis, size, bit)
        kept = jnp.where(upper, high, low)
        found = jnp.concatenate([jnp.where(upper, got, kept), jnp.where(upper, kept, got)], 1)
        bit //= 2
    return found[0]


def in_order(first, then):
    return lax.optimization_barrier((first, then))


def per_device(n_row, n_col, trailing, panel_block, diag_block, tile_map):
    slots, rows, n = panel_block.shape
    tile = rows * n_col
    row, col = lax.axis_index("row"), lax.axis_index("col")
    core = col & 1
    slot_index = jnp.arange(tile_map.shape[0], dtype=jnp.int32)
    own_tiles = lax.dynamic_slice_in_dim(tile_map, row * slots, slots)
    live = (own_tiles >= col).astype(jnp.int32)
    where = jnp.concatenate([jnp.stack([row, col, core]).astype(jnp.int32), live])
    row_bits, col_bits = bits_of(n_row), bits_of(n_col)
    owner = jnp.stack([jnp.sum(jnp.where(tile_map == c, slot_index, 0)) for c in range(n_col)])

    half = n // n_row // 2
    side = lax.dynamic_slice_in_dim(diag_block, core * half, half, 0)
    if packed(n, n_row):
        side = lax.dynamic_slice_in_dim(jnp.concatenate([side, side], 1), row * BLOCK, (n_row // 2 + 1) * BLOCK, 1)
    side = side[None]

    held = {"parts": panel_block, "stage": 0}

    def halve():
        stage = held["stage"]
        bit, parts = 1 << stage, held["parts"]
        upper = (row >> stage) & 1
        length = parts.shape[1] // 2
        got = flip(lax.dynamic_slice_in_dim(parts, (1 - upper) * length, length, 1), "row", n_row, bit)
        kept = lax.dynamic_slice_in_dim(parts, upper * length, length, 1)
        chosen = held.get("chosen")
        if chosen is None:
            both = jnp.where(upper > 0, jnp.stack([got, kept]), jnp.stack([kept, got]))
            parts = both.reshape((2 * parts.shape[0],) + kept.shape[1:])
            if parts.shape[0] > n_col:
                base = (row >> (stage + 1)) * parts.shape[0]
                picks = [lax.dynamic_index_in_dim(parts, owner[c] - base, 0, keepdims=False) for c in range(n_col)]
                parts = jnp.stack(picks)
                held["chosen"] = True
        elif chosen == "own":
            ours = (owner[col] // slots) >> stage == row >> stage
            parts = jnp.where(ours, kept, got)
        else:
            ours = (owner // slots) >> stage == row >> stage
            parts = jnp.where(ours[:, None, None], kept, got)
        held["parts"], held["stage"] = parts, stage + 1

    found = {0: panel_block, col_bits[0]: flip(panel_block, "col", n_col, col_bits[0])}
    for bit in row_bits[:-1]:
        side = grow(side, "row", n_row, bit)
    halve()
    side, held["parts"] = in_order(side, held["parts"])
    side = grow(side, "row", n_row, row_bits[-1])
    for _ in row_bits[1:-1]:
        halve()
    diag = (side, flip(side, "col", n_col, 1))
    found[col_bits[0]], held["parts"] = in_order(found[col_bits[0]], held["parts"])
    for bit in col_bits[1:]:
        for p in list(found):
            found[p | bit] = flip(found[p], "col", n_col, bit)
    held["parts"] = swap(held["parts"], "col", n_col)
    held["chosen"] = "own"
    *diag, held["parts"] = lax.optimization_barrier((*diag, held["parts"]))
    halve()
    column = held["parts"][None]

    state, wh, wl = [], [], []
    bits = list(row_bits)
    for k in range(n // WIDE):
        state, h, low = cholesky_pair(k, n, n_row, where, diag, state)
        wh.append(h)
        wl.append(low)
        if k + 1 < n // WIDE:
            *state, column = lax.optimization_barrier((*state, column))
            for bit in bits[: max(1, len(bits) - (n // WIDE - 2 - k))]:
                column = grow(column, "row", n_row, bit)
                bits = bits[1:]

    chunk = rows // n_row
    if chunk % 8 == 0:
        column = column.reshape(n_row * n_col, chunk, n)

        def places(at):
            me = flipped_place(at, n_row)
            return [(q ^ me) * n_col + flipped_place(j, n_col) for j in range(n_col) for q in range(n_row)]
    else:
        order = jnp.arange(n_row, dtype=jnp.int32) ^ flipped_place(row, n_row)
        swapped = jnp.array([flipped_place(j, n_col) for j in range(n_col)])
        column = column[order][:, swapped].transpose(1, 0, 2, 3).reshape(tile // 8, 8, n)

        def places(at):
            return list(range(tile // 8))

    row_pieces = [found[p] for p in range(n_col)]
    panel_factor, diag_factor, lh, ll, xh, xl = factor_rows(where, row_pieces, state[-1], wh, wl, n_row)
    updated = update(where, n_col, column, places, lh, ll, wh, wl, xh, xl, trailing)
    return updated, panel_factor, diag_factor


def solution(mesh):
    n_row, n_col = mesh.shape["row"], mesh.shape["col"]
    in_specs = (P("row", "col", None, None), P("row", "col", None), P("row", None), P())
    out_specs = (P("row", "col", None, None), P("row", "col", None), P("row", None))
    return jax.shard_map(
        functools.partial(per_device, n_row, n_col),
        mesh=mesh,
        in_specs=in_specs,
        out_specs=out_specs,
        check_vma=False,
    )
```

```python
import functools

import jax
import jax.numpy as jnp
from jax import lax
from jax.experimental import pallas as pl
from jax.experimental.pallas import tpu as pltpu
from jax.sharding import PartitionSpec as P

BLOCK = 128
WIDE = 256
F32, BF16 = jnp.float32, jnp.bfloat16


def spread_row(x, m):
    return jnp.broadcast_to(x[m : m + 1, :], x.shape)


def spread_lane(x, j):
    return jnp.broadcast_to(x[:, j : j + 1], x.shape)


def factor_block(rows_in, between):
    count = len(rows_in)
    work = list(rows_in)
    lane = lax.broadcasted_iota(jnp.int32, (8, BLOCK), 1)
    sub = lax.broadcasted_iota(jnp.int32, (8, BLOCK), 0)
    upper, inverse = [], []
    for b in range(count):
        between(b)
        o = 8 * b
        rows = [spread_row(work[b], m) for m in range(8)]
        p = {(m, l): spread_lane(rows[m], o + l) for m in range(8) for l in range(m + 1)}
        r = list(rows)
        t = [jnp.where(lane == o + m, 1.0, jnp.where(lane >= o, 0.0, rows[m])) for m in range(8)]
        inside = (lane >= o) & (lane < o + 8)
        following = None
        if b + 1 < count:
            c = [spread_lane(work[b + 1], o + m) for m in range(8)]
            following = jnp.where(inside, 0.0, work[b + 1])
        f, ri = {}, []
        for j in range(8):
            ri.append(pl.reciprocal(p[j, j], approx=True))
            for m in range(j + 1, 8):
                f[m, j] = p[m, j] * ri[j]
                for l in range(j + 1, m + 1):
                    if m == j + 1:
                        p[m, l] = p[m, l] - (p[m, j] * p[l, j]) * ri[j]
                    else:
                        p[m, l] = p[m, l] - f[m, j] * p[l, j]
                r[m] = r[m] - f[m, j] * r[j]
                t[m] = t[m] - f[m, j] * t[j]
            if following is not None:
                following = following - c[j] * (jnp.where(lane < o + 8, t[j], r[j]) * ri[j])
                for m in range(j + 1, 8):
                    c[m] = c[m] - c[j] * f[m, j]
        up, inv = None, None
        for m in range(8):
            s = lax.rsqrt(p[m, m])
            um, im = r[m] * s, t[m] * s
            up = um if m == 0 else jnp.where(sub == m, um, up)
            inv = im if m == 0 else jnp.where(sub == m, im, inv)
        upper.append(jnp.where(lane >= sub + o, up, 0.0))
        inverse.append(inv)
        if following is not None:
            work[b + 1] = following
        if b + 2 < count:
            z = [None] * 8
            for m in range(7, -1, -1):
                v = jnp.where(lane < o + 8, t[m], r[m]) * ri[m]
                for l in range(7, m, -1):
                    v = v - f[l, m] * z[l]
                z[m] = v
            for i in range(b + 2, count):
                v = jnp.where(inside, 0.0, work[i])
                for m in range(8):
                    v = v - spread_lane(work[i], o + m) * z[m]
                work[i] = v
    return upper, inverse


def dot_nt(a, b, precision=None):
    return lax.dot_general(a, b, (((1,), (1,)), ((), ())), precision=precision, preferred_element_type=F32)


def full_nt(a, b):
    return dot_nt(a, b, lax.Precision.HIGHEST)


def halves(x):
    high = x.astype(BF16)
    return high, (x - high.astype(F32)).astype(BF16)


def split_nt(ah, al, bh, bl):
    return dot_nt(ah, bh) + (dot_nt(ah, bl) + dot_nt(al, bh))


def flipped_place(index, count):
    place, bit = 0, 1
    while bit < count:
        place = place * 2 + (index & 1)
        index = index >> 1
        bit *= 2
    return place


def packed(n, n_row):
    return n_row * BLOCK == n


def window_block(row, d, n, n_row):
    return (row + d) % n_row if packed(n, n_row) else d


def own_vmem():
    return pl.BlockSpec(memory_space=pltpu.VMEM)


def pair_kernel(pair, n, n_row, *refs):
    count, last = n // BLOCK, pair * WIDE + WIDE == n
    start, end = 2 * pair * BLOCK, 2 * pair * BLOCK + WIDE
    refs = list(refs)

    def take(number):
        taken = refs[:number]
        del refs[:number]
        return taken

    if pair:
        win_ref, d_in, s_in, w0_in, w1_in, _ = take(6)
    else:
        (where_ref,) = take(1)
        diag_ref = take(1)[0]
        pieces = take(2 * n_row - 2)
        (win_ref,) = take(1)
    (l_ref,) = take(1)
    if pair:
        wide_refs = take(2)
    if last:
        final_refs = take(2)
    else:
        d_out, s_out, *w_out = take(4)
    s_ref, d_ref, w_ref, piece_sem = refs

    def block(i, k):
        if packed(n, n_row):
            if 0 < i - k < n_row // 2:
                return win_ref[k, :, (i - k) * BLOCK : (i - k + 1) * BLOCK].T
            d = (k - i) % n_row
            return win_ref[i, :, d * BLOCK : (d + 1) * BLOCK]
        share = n // n_row
        parts = [win_ref[g, :, k * BLOCK : (k + 1) * BLOCK] for g in range(i * BLOCK // share, (i + 1) * BLOCK // share)]
        return jnp.concatenate(parts, 0)

    def at(i):
        return slice(i * BLOCK, i * BLOCK + BLOCK)

    def rest_of_factor(i, k):
        def work():
            source = s_in[at(i), :] if pair and k < 2 * pair else s_ref[k % 2, at(i), :]
            inverse = w1_in[...] if pair and k < 2 * pair else w_ref[k % 2]
            l_ref[at(i), at(k)] = full_nt(source, inverse)

        return work

    def below(i, k):
        def work():
            value = block(i, k)
            if k:
                value = value - full_nt(l_ref[at(i), : k * BLOCK], l_ref[at(k), : k * BLOCK])
            s_ref[k % 2, at(i), :] = value

        return work

    def next_diagonal(k):
        def work():
            value = block(k, k)
            if k > 1:
                value = value - full_nt(l_ref[at(k), : (k - 1) * BLOCK], l_ref[at(k), : (k - 1) * BLOCK])
            d_ref[...] = value

        return work

    def widen(first, second, cross, high_ref, low_ref):
        mixed = jnp.dot(cross, first, precision=lax.Precision.HIGHEST, preferred_element_type=F32)
        corner = -jnp.dot(second, mixed, precision=lax.Precision.HIGHEST, preferred_element_type=F32)
        whole = jnp.concatenate(
            [jnp.concatenate([first, jnp.zeros_like(first)], 1), jnp.concatenate([corner, second], 1)], 0
        )
        high_ref[...], low_ref[...] = halves(whole)

    if not pair:
        row, core = where_ref[0], where_ref[2]
        share = n // n_row
        half = share // 2
        copies = []
        for d in range(win_ref.shape[2] // BLOCK):
            source = pl.ds(pl.multiple_of(window_block(row, d, n, n_row) * BLOCK, BLOCK), BLOCK)
            target = win_ref.at[row, :, pl.ds(d * BLOCK, BLOCK)]
            copies.append(pltpu.make_async_copy(diag_ref.at[:, source], target, piece_sem.at[row]))
        for i, piece in enumerate(pieces):
            g = row ^ (i // 2 + 1)
            target = win_ref.at[g, pl.ds(pl.multiple_of((core ^ (i % 2)) * half, half), half), :]
            copies.append(pltpu.make_async_copy(piece, target, piece_sem.at[g]))
        for copy in copies:
            copy.start()

    def arrive(g):
        pltpu.make_async_copy(win_ref.at[g], win_ref.at[g], piece_sem.at[g]).wait()

    for k in range(2 * pair, 2 * pair + 2):
        tasks = []
        for i in range(k + 1, count):
            if k:
                tasks.append(rest_of_factor(i, k - 1))
            tasks.append(below(i, k))
        if k + 1 < count:
            tasks.append(next_diagonal(k + 1))
        if pair and k == 2 * pair:
            tasks.append(lambda: widen(w0_in[...], w1_in[...], l_ref[at(k - 1), at(k - 2)], *wide_refs))

        def between(b):
            if b == 3 and k == 0:
                for g in range(BLOCK // share, n_row):
                    arrive(g)
            if b >= (1 if k else 3):
                left = BLOCK // 8 - b
                for _ in range(-(-len(tasks) // left)):
                    tasks.pop(0)()

        if k == 0:
            for g in range(BLOCK // share):
                arrive(g)
            source = block(0, 0)
        elif k == 2 * pair:
            source = d_in[...]
        else:
            source = d_ref[...]
        upper, inverse = factor_block([source[8 * j : 8 * j + 8, :] for j in range(BLOCK // 8)], between)
        inverse = jnp.concatenate(inverse, 0)
        w_ref[k % 2] = inverse
        l_ref[at(k), at(k)] = jnp.concatenate(upper, 0).T
        if k + 1 < count:
            cross = full_nt(s_ref[k % 2, at(k + 1), :], inverse)
            l_ref[at(k + 1), at(k)] = cross
            value = d_ref[...] - full_nt(cross, cross)
            if k % 2:
                d_out[...] = value
            else:
                d_ref[...] = value
    if last:
        widen(w_ref[0], w_ref[1], l_ref[at(count - 1), at(count - 2)], *final_refs)
    else:
        s_out[...] = s_ref[1]
        w_out[0][...] = w_ref[0]
        w_out[1][...] = w_ref[1]


def cholesky_pair(pair, n, n_row, where, state):
    anywhere = pl.BlockSpec(memory_space=pl.ANY)
    last = pair * WIDE + WIDE == n
    small = jax.ShapeDtypeStruct((BLOCK, BLOCK), F32)
    square = jax.ShapeDtypeStruct((WIDE, WIDE), BF16)
    shapes, out_specs = [], []
    if not pair:
        window = state[1].shape[1]
        shapes.append(jax.ShapeDtypeStruct((n_row, n // n_row, window), F32))
        out_specs.append(own_vmem())
    shapes.append(jax.ShapeDtypeStruct((n, n), F32))
    out_specs.append(own_vmem())
    wide = [square] * (2 * (pair > 0) + 2 * last)
    kept = [] if last else [small, jax.ShapeDtypeStruct((n, BLOCK), F32), small, small]
    shapes += wide + kept
    out_specs += [own_vmem()] * len(wide + kept)
    out = pl.pallas_call(
        functools.partial(pair_kernel, pair, n, n_row),
        out_shape=shapes,
        in_specs=[own_vmem()] * 6 if pair else [pl.BlockSpec(memory_space=pltpu.SMEM)] + [anywhere] * len(state),
        out_specs=out_specs,
        input_output_aliases={5: 0} if pair else {},
        scratch_shapes=[
            pltpu.VMEM((2, n, BLOCK), F32),
            pltpu.VMEM((BLOCK, BLOCK), F32),
            pltpu.VMEM((2, BLOCK, BLOCK), F32),
            pltpu.SemaphoreType.DMA((n_row,)),
        ],
        compiler_params=pltpu.CompilerParams(vmem_limit_bytes=16 * 2**20),
        cost_estimate=pl.CostEstimate(flops=14_000_000_000, bytes_accessed=4 * n * BLOCK * 4, transcendentals=0),
        name=f"cholesky_{pair}",
    )(*([] if pair else [where]), *state)
    window = state[0] if pair else out[0]
    l, *out = out if pair else out[1:]
    wide, kept = out[: len(wide)], out[len(wide) :]
    return [window, *kept, l], wide


def solve(source, xh_ref, xl_ref, lh_ref, ll_ref, wh_ref, wl_ref, keep_ref=None):
    n = lh_ref.shape[0]
    for k in range(n // WIDE):
        lo, hi = k * WIDE, k * WIDE + WIDE
        rest = source[:, lo:hi]
        if k:
            rest = rest - split_nt(xh_ref[:, :lo], xl_ref[:, :lo], lh_ref[lo:hi, :lo], ll_ref[lo:hi, :lo])
        rh, rl = halves(rest)
        x = split_nt(rh, rl, wh_ref[k][...], wl_ref[k][...])
        if keep_ref is not None:
            keep_ref[:, lo:hi] = x
        xh_ref[:, lo:hi], xl_ref[:, lo:hi] = halves(x)


def rows_kernel(n_row, n_piece, where_ref, *refs):
    pieces, l_ref = refs[:n_piece], refs[n_piece]
    slots, rows, n = pieces[0].shape
    count, wide = n // BLOCK, n // WIDE
    refs = refs[n_piece + 1 :]
    wh_ref, wl_ref = refs[:wide], refs[wide : 2 * wide]
    own_ref, diag_ref, lh_ref, ll_ref, xh_ref, xl_ref, p_ref, p_sem = refs[2 * wide :]
    row, col = where_ref[0], where_ref[1]
    many = slots * rows
    p_copies = []
    for i in range(n_piece):
        for t in range(slots):
            at = pl.multiple_of((col ^ i) * many + t * rows, rows)
            p_copies.append(
                pltpu.make_async_copy(pieces[i].at[t], p_ref.at[pl.ds(at, rows), :], p_sem.at[i * slots + t])
            )
    for copy in p_copies:
        copy.start()
    for k in range(count):
        lo, hi = k * BLOCK, k * BLOCK + BLOCK
        lh_ref[lo:, lo:hi], ll_ref[lo:, lo:hi] = halves(l_ref[lo:, lo:hi])
    share = n // n_row
    mine = l_ref[pl.ds(pl.multiple_of(row * share, share), share), :]
    block = lax.broadcasted_iota(jnp.int32, mine.shape, 1) // BLOCK
    diag_ref[...] = jnp.where(block <= row * share // BLOCK, mine, jnp.zeros_like(mine))
    for copy in p_copies:
        copy.wait()
    batch = 512

    @pl.loop(0, n_piece * many // batch)
    def _(i):
        at = pl.ds(pl.multiple_of(i * batch, batch), batch)
        solve(p_ref.at[at, :], xh_ref.at[at, :], xl_ref.at[at, :], lh_ref, ll_ref, wh_ref, wl_ref, p_ref.at[at, :])

    own_ref[...] = p_ref[pl.ds(pl.multiple_of(col * many, many), many), :].reshape(slots, rows, n)


def factor_rows(where, pieces, l, wh, wl, n_row):
    count = len(pieces)
    slots, rows, n = pieces[0].shape
    total = count * slots * rows
    anywhere = pl.BlockSpec(memory_space=pl.ANY)
    return pl.pallas_call(
        functools.partial(rows_kernel, n_row, count),
        out_shape=(
            jax.ShapeDtypeStruct((slots, rows, n), F32),
            jax.ShapeDtypeStruct((n // n_row, n), F32),
            jax.ShapeDtypeStruct((n, n), BF16),
            jax.ShapeDtypeStruct((n, n), BF16),
            jax.ShapeDtypeStruct((total, n), BF16),
            jax.ShapeDtypeStruct((total, n), BF16),
        ),
        in_specs=[pl.BlockSpec(memory_space=pltpu.SMEM)] + [anywhere] * count + [own_vmem()] * (1 + len(wh) + len(wl)),
        out_specs=[own_vmem()] * 6,
        scratch_shapes=[
            pltpu.VMEM((total, n), F32),
            pltpu.SemaphoreType.DMA((count * slots,)),
        ],
        compiler_params=pltpu.CompilerParams(vmem_limit_bytes=20 * 2**20),
        cost_estimate=pl.CostEstimate(flops=10_000_000_000, bytes_accessed=20 * n * n, transcendentals=0),
        name="factor_rows",
    )(where, *pieces, l, *wh, *wl)


def update_kernel(n_piece, places, where_ref, map_ref, g_ref, lh_ref, ll_ref, xh_ref, xl_ref, t_ref, *refs):
    wide = g_ref.shape[2] // WIDE
    wh_ref, wl_ref = refs[:wide], refs[wide : 2 * wide]
    out_ref, p_ref, ch_ref, cl_ref = refs[2 * wide :]
    slots, _, tile, _ = t_ref.shape
    rows = tile // n_piece
    row, col = where_ref[0], where_ref[1]
    chunk = g_ref.shape[1]
    for i, at in enumerate(places(row)):
        p_ref[i * chunk : i * chunk + chunk, :] = g_ref[at]
    solve(p_ref, ch_ref, cl_ref, lh_ref, ll_ref, wh_ref, wl_ref)

    @pl.loop(0, n_piece)
    def _(i):
        at = pl.ds(pl.multiple_of(i * rows, rows), rows)
        many = pl.ds(pl.multiple_of(i * (slots * rows), slots * rows), slots * rows)
        product = split_nt(xh_ref[many, :], xl_ref[many, :], ch_ref[...], cl_ref[...])
        for s in range(slots):
            live = map_ref[row * slots + s] >= col
            new = t_ref[s, 0, at, :] - product[s * rows : (s + 1) * rows]
            out_ref[s, 0, at, :] = jnp.where(live, new, jnp.zeros_like(new))


def update(where, tile_map, n_piece, gathered, places, lh, ll, wh, wl, xh, xl, trailing):
    tile = trailing.shape[2]
    n = gathered.shape[2]
    return pl.pallas_call(
        functools.partial(update_kernel, n_piece, places),
        out_shape=jax.ShapeDtypeStruct(trailing.shape, F32),
        in_specs=[pl.BlockSpec(memory_space=pltpu.SMEM)] * 2 + [own_vmem()] * (6 + len(wh) + len(wl)),
        out_specs=own_vmem(),
        scratch_shapes=[pltpu.VMEM((tile, n), F32), pltpu.VMEM((tile, n), BF16), pltpu.VMEM((tile, n), BF16)],
        compiler_params=pltpu.CompilerParams(vmem_limit_bytes=20 * 2**20),
        cost_estimate=pl.CostEstimate(flops=10_000_000_000, bytes_accessed=20 * n * n, transcendentals=0),
        name="update",
    )(where, tile_map, gathered, lh, ll, xh, xl, trailing, *wh, *wl)


def flip(x, axis, size, bit):
    return lax.ppermute(x, axis, [(i, i ^ bit) for i in range(size)])


def grow(x, axis, size, bit):
    return jnp.concatenate([x, flip(x, axis, size, bit)], 0)


def fan_out(found, bits, size):
    out = dict(found)
    for bit in bits:
        for p in found:
            out[p | bit] = flip(found[p], "row", size, bit)
    return out


def bits_of(size):
    return [size >> i for i in range(1, size.bit_length())]


def swap(x, axis, size):
    me = lax.axis_index(axis)
    found = x.reshape((size, 1) + x.shape[1:])
    bit = size // 2
    while bit:
        width = found.shape[0] // 2
        upper = (me & bit) > 0
        low, high = found[:width], found[width:]
        got = flip(jnp.where(upper, low, high), axis, size, bit)
        kept = jnp.where(upper, high, low)
        found = jnp.concatenate([jnp.where(upper, got, kept), jnp.where(upper, kept, got)], 1)
        bit //= 2
    return found[0]


def in_order(first, then):
    return lax.optimization_barrier((first, then))


def per_device(n_row, n_col, trailing, panel_block, diag_block, tile_map):
    slots, rows, n = panel_block.shape
    tile = rows * n_col
    row, col = lax.axis_index("row"), lax.axis_index("col")
    core = col & 1
    slot_index = jnp.arange(tile_map.shape[0], dtype=jnp.int32)
    where = jnp.stack([row, col, core]).astype(jnp.int32)
    row_bits, col_bits = bits_of(n_row), bits_of(n_col)
    owner = jnp.sum(jnp.where(tile_map[None] == jnp.arange(n_col, dtype=jnp.int32)[:, None], slot_index[None], 0), 1)
    own_owner = jnp.sum(jnp.where(tile_map == col, slot_index, 0))

    half = n // n_row // 2
    width = (n_row // 2 + 1) * BLOCK if packed(n, n_row) else n
    side = lax.dynamic_slice_in_dim(diag_block, core * half, half, 0)
    if packed(n, n_row):
        side = lax.dynamic_slice_in_dim(jnp.concatenate([side, side], 1), row * BLOCK, width, 1)

    held = {"parts": panel_block, "stage": 0}

    def halve():
        stage = held["stage"]
        bit, parts = 1 << stage, held["parts"]
        upper = (row >> stage) & 1
        length = parts.shape[1] // 2
        got = flip(lax.dynamic_slice_in_dim(parts, (1 - upper) * length, length, 1), "row", n_row, bit)
        kept = lax.dynamic_slice_in_dim(parts, upper * length, length, 1)
        chosen = held.get("chosen")
        if chosen is None:
            both = jnp.where(upper > 0, jnp.stack([got, kept]), jnp.stack([kept, got]))
            parts = both.reshape((2 * parts.shape[0],) + kept.shape[1:])
            if parts.shape[0] > n_col:
                base = (row >> (stage + 1)) * parts.shape[0]
                picks = [lax.dynamic_index_in_dim(parts, owner[c] - base, 0, keepdims=False) for c in range(n_col)]
                parts = jnp.stack(picks)
                held["chosen"] = True
        elif chosen == "own":
            ours = (own_owner // slots) >> stage == row >> stage
            parts = jnp.where(ours, kept, got)
        else:
            ours = (owner // slots) >> stage == row >> stage
            parts = jnp.where(ours[:, None, None], kept, got)
        held["parts"], held["stage"] = parts, stage + 1

    mine = {0: side}
    for bit in row_bits:
        for p in list(mine):
            mine[p | bit] = flip(mine[p], "row", n_row, bit)
    found = {0: panel_block, col_bits[0]: flip(panel_block, "col", n_col, col_bits[0])}
    halve()
    for level in range(1, len(row_bits)):
        early = [p for p in mine if bin(p).count("1") == level]
        *some, held["parts"] = lax.optimization_barrier((*[mine[p] for p in early], held["parts"]))
        mine.update(zip(early, some))
        halve() if level + 1 < len(row_bits) else None
    diag = [diag_block]
    for p in range(1, n_row):
        diag += [mine[p], flip(mine[p], "col", n_col, 1)]
    found[col_bits[0]], held["parts"] = in_order(found[col_bits[0]], held["parts"])
    held["parts"] = swap(held["parts"], "col", n_col)
    held["chosen"] = "own"
    *diag, held["parts"] = lax.optimization_barrier((*diag, held["parts"]))
    halve()
    column = held["parts"][None]

    state, wide = diag, []
    together = {0: column[0]}
    bits = list(row_bits)
    for k in range(n // WIDE):
        state, more = cholesky_pair(k, n, n_row, where, state)
        wide += more
        if k + 1 < n // WIDE:
            *state, last = lax.optimization_barrier((*state, together[max(together)]))
            together[max(together)] = last
            if k == 1:
                together = fan_out(together, bits, n_row)
            elif k == 0:
                for bit in bits[:-2]:
                    for p in list(together):
                        together[p | bit] = flip(together[p], "row", n_row, bit)
                bits = bits[-2:]
            else:
                for p in [p for p in together if p & bits[0] and not p & bits[1]]:
                    together[p | bits[1]] = flip(together[p], "row", n_row, bits[1])
        if k == n // WIDE - 2:
            *state, found[col_bits[0]] = lax.optimization_barrier((*state, found[col_bits[0]]))
            for bit in col_bits[1:]:
                for p in list(found):
                    found[p | bit] = flip(found[p], "col", n_col, bit)
    wh, wl = wide[::2], wide[1::2]
    row_pieces = [found[p] for p in range(n_col)]
    panel_factor, diag_factor, lh, ll, xh, xl = factor_rows(where, row_pieces, state[-1], wh, wl, n_row)
    xh, together[0] = in_order(xh, together[0])
    column = jnp.stack([together[flipped_place(p, n_row)] for p in range(n_row)])

    chunk = rows // n_row
    if chunk % 8 == 0:
        column = column.reshape(n_row * n_col, chunk, n)

        def places(at):
            me = flipped_place(at, n_row)
            return [(q ^ me) * n_col + flipped_place(j, n_col) for j in range(n_col) for q in range(n_row)]
    else:
        order = jnp.arange(n_row, dtype=jnp.int32) ^ flipped_place(row, n_row)
        swapped = jnp.array([flipped_place(j, n_col) for j in range(n_col)])
        column = column[order][:, swapped].transpose(1, 0, 2, 3).reshape(tile // 8, 8, n)

        def places(at):
            return list(range(tile // 8))

    updated = update(where, tile_map, n_col, column, places, lh, ll, wh, wl, xh, xl, trailing)
    return updated, panel_factor, diag_factor


def solution(mesh):
    n_row, n_col = mesh.shape["row"], mesh.shape["col"]
    in_specs = (P("row", "col", None, None), P("row", "col", None), P("row", None), P())
    out_specs = (P("row", "col", None, None), P("row", "col", None), P("row", None))
    return jax.shard_map(
        functools.partial(per_device, n_row, n_col),
        mesh=mesh,
        in_specs=in_specs,
        out_specs=out_specs,
        check_vma=False,
    )
```

```python
import functools

import jax
import jax.numpy as jnp
from jax import lax
from jax.experimental import pallas as pl
from jax.experimental.pallas import tpu as pltpu
from jax.sharding import PartitionSpec as P

BLOCK = 128
WIDE = 256
F32, BF16 = jnp.float32, jnp.bfloat16


def spread_row(x, m):
    return jnp.broadcast_to(x[m : m + 1, :], x.shape)


def spread_lane(x, j):
    return jnp.broadcast_to(x[:, j : j + 1], x.shape)


def factor_block(rows_in, between):
    count = len(rows_in)
    work = list(rows_in)
    lane = lax.broadcasted_iota(jnp.int32, (8, BLOCK), 1)
    sub = lax.broadcasted_iota(jnp.int32, (8, BLOCK), 0)
    upper, inverse = [], []
    for b in range(count):
        between(b)
        o = 8 * b
        rows = [spread_row(work[b], m) for m in range(8)]
        p = {(m, l): spread_lane(rows[m], o + l) for m in range(8) for l in range(m + 1)}
        r = list(rows)
        t = [jnp.where(lane == o + m, 1.0, jnp.where(lane >= o, 0.0, rows[m])) for m in range(8)]
        inside = (lane >= o) & (lane < o + 8)
        following = None
        if b + 1 < count:
            c = [spread_lane(work[b + 1], o + m) for m in range(8)]
            following = jnp.where(inside, 0.0, work[b + 1])
        f, ri = {}, []
        for j in range(8):
            ri.append(pl.reciprocal(p[j, j], approx=True))
            for m in range(j + 1, 8):
                f[m, j] = p[m, j] * ri[j]
                for l in range(j + 1, m + 1):
                    if m == j + 1:
                        p[m, l] = p[m, l] - (p[m, j] * p[l, j]) * ri[j]
                    else:
                        p[m, l] = p[m, l] - f[m, j] * p[l, j]
                r[m] = r[m] - f[m, j] * r[j]
                t[m] = t[m] - f[m, j] * t[j]
            if following is not None:
                following = following - c[j] * (jnp.where(lane < o + 8, t[j], r[j]) * ri[j])
                for m in range(j + 1, 8):
                    c[m] = c[m] - c[j] * f[m, j]
        up, inv = None, None
        for m in range(8):
            s = lax.rsqrt(p[m, m])
            um, im = r[m] * s, t[m] * s
            up = um if m == 0 else jnp.where(sub == m, um, up)
            inv = im if m == 0 else jnp.where(sub == m, im, inv)
        upper.append(jnp.where(lane >= sub + o, up, 0.0))
        inverse.append(inv)
        if following is not None:
            work[b + 1] = following
        if b + 2 < count:
            z = [None] * 8
            for m in range(7, -1, -1):
                v = jnp.where(lane < o + 8, t[m], r[m]) * ri[m]
                for l in range(7, m, -1):
                    v = v - f[l, m] * z[l]
                z[m] = v
            for i in range(b + 2, count):
                v = jnp.where(inside, 0.0, work[i])
                for m in range(8):
                    v = v - spread_lane(work[i], o + m) * z[m]
                work[i] = v
    return upper, inverse


def dot_nt(a, b, precision=None):
    return lax.dot_general(a, b, (((1,), (1,)), ((), ())), precision=precision, preferred_element_type=F32)


def full_nt(a, b):
    return dot_nt(a, b, lax.Precision.HIGHEST)


def halves(x):
    high = x.astype(BF16)
    return high, (x - high.astype(F32)).astype(BF16)


def split_nt(ah, al, bh, bl):
    return dot_nt(ah, bh) + (dot_nt(ah, bl) + dot_nt(al, bh))


def flipped_place(index, count):
    place, bit = 0, 1
    while bit < count:
        place = place * 2 + (index & 1)
        index = index >> 1
        bit *= 2
    return place


def packed(n, n_row):
    return n_row * BLOCK == n


def window_block(row, d, n, n_row):
    return (row + d) % n_row if packed(n, n_row) else d


def own_vmem():
    return pl.BlockSpec(memory_space=pltpu.VMEM)


def pair_kernel(pair, n, n_row, n_piece, *refs):
    count, last = n // BLOCK, pair * WIDE + WIDE == n
    start, end = 2 * pair * BLOCK, 2 * pair * BLOCK + WIDE
    refs = list(refs)

    def take(number):
        taken = refs[:number]
        del refs[:number]
        return taken

    if pair:
        win_ref, d_in, s_in, w0_in, w1_in, _ = take(6)
        if pair == 1:
            (where_ref,) = take(1)
            panels = take(n_piece)
        else:
            take(5)
    else:
        (where_ref,) = take(1)
        diag_ref = take(1)[0]
        pieces = take(2 * n_row - 2)
        (win_ref,) = take(1)
    (l_ref,) = take(1)
    if pair:
        x_ref, xh_ref, xl_ref, lh_ref, ll_ref = take(5)
        wide_refs = take(2)
    if last:
        final_refs = take(2)
    else:
        d_out, s_out, *w_out = take(4)
    s_ref, d_ref, w_ref, piece_sem = refs

    def block(i, k):
        if packed(n, n_row):
            if 0 < i - k < n_row // 2:
                return win_ref[k, :, (i - k) * BLOCK : (i - k + 1) * BLOCK].T
            d = (k - i) % n_row
            return win_ref[i, :, d * BLOCK : (d + 1) * BLOCK]
        share = n // n_row
        parts = [win_ref[g, :, k * BLOCK : (k + 1) * BLOCK] for g in range(i * BLOCK // share, (i + 1) * BLOCK // share)]
        return jnp.concatenate(parts, 0)

    def at(i):
        return slice(i * BLOCK, i * BLOCK + BLOCK)

    def rest_of_factor(i, k):
        def work():
            source = s_in[at(i), :] if pair and k < 2 * pair else s_ref[k % 2, at(i), :]
            inverse = w1_in[...] if pair and k < 2 * pair else w_ref[k % 2]
            l_ref[at(i), at(k)] = full_nt(source, inverse)

        return work

    def below(i, k):
        def work():
            value = block(i, k)
            if k:
                value = value - full_nt(l_ref[at(i), : k * BLOCK], l_ref[at(k), : k * BLOCK])
            s_ref[k % 2, at(i), :] = value

        return work

    def next_diagonal(k):
        def work():
            value = block(k, k)
            if k > 1:
                value = value - full_nt(l_ref[at(k), : (k - 1) * BLOCK], l_ref[at(k), : (k - 1) * BLOCK])
            d_ref[...] = value

        return work

    def widen(first, second, cross, high_ref, low_ref):
        mixed = jnp.dot(cross, first, precision=lax.Precision.HIGHEST, preferred_element_type=F32)
        corner = -jnp.dot(second, mixed, precision=lax.Precision.HIGHEST, preferred_element_type=F32)
        whole = jnp.concatenate(
            [jnp.concatenate([first, jnp.zeros_like(first)], 1), jnp.concatenate([corner, second], 1)], 0
        )
        high_ref[...], low_ref[...] = halves(whole)

    panel_copies = []
    if pair == 1:
        slots, rows, _ = panels[0].shape
        for i, panel in enumerate(panels):
            for t in range(slots):
                first = pl.multiple_of(((where_ref[1] ^ i) * slots + t) * rows, rows)
                target = x_ref.at[pl.ds(first, rows), :]
                panel_copies.append(pltpu.make_async_copy(panel.at[t], target, piece_sem.at[i * slots + t]))
        for copy in panel_copies:
            copy.start()

    before = slice(start - WIDE, start)

    def split_factor():
        lh_ref[before, :start], ll_ref[before, :start] = halves(l_ref[before, :start])

    def solve_panel(first):
        def work():
            those = slice(first, first + WIDE)
            rest = x_ref[those, before]
            if pair > 1:
                done = slice(0, start - WIDE)
                rest = rest - split_nt(xh_ref[those, done], xl_ref[those, done], lh_ref[before, done], ll_ref[before, done])
            x = split_nt(*halves(rest), wide_refs[0][...], wide_refs[1][...])
            x_ref[those, before] = x
            xh_ref[those, before], xl_ref[those, before] = halves(x)

        return work

    if not pair:
        row, core = where_ref[0], where_ref[2]
        share = n // n_row
        half = share // 2
        copies = []
        for d in range(win_ref.shape[2] // BLOCK):
            source = pl.ds(pl.multiple_of(window_block(row, d, n, n_row) * BLOCK, BLOCK), BLOCK)
            target = win_ref.at[row, :, pl.ds(d * BLOCK, BLOCK)]
            copies.append(pltpu.make_async_copy(diag_ref.at[:, source], target, piece_sem.at[row]))
        for i, piece in enumerate(pieces):
            g = row ^ (i // 2 + 1)
            target = win_ref.at[g, pl.ds(pl.multiple_of((core ^ (i % 2)) * half, half), half), :]
            copies.append(pltpu.make_async_copy(piece, target, piece_sem.at[g]))
        for copy in copies:
            copy.start()

    def arrive(g):
        pltpu.make_async_copy(win_ref.at[g], win_ref.at[g], piece_sem.at[g]).wait()

    for k in range(2 * pair, 2 * pair + 2):
        tasks = []
        for i in range(k + 1, count):
            if k:
                tasks.append(rest_of_factor(i, k - 1))
            tasks.append(below(i, k))
        if k + 1 < count:
            tasks.append(next_diagonal(k + 1))
        if pair and k == 2 * pair:
            tasks.append(lambda: widen(w0_in[...], w1_in[...], l_ref[at(k - 1), at(k - 2)], *wide_refs))
            tasks.append(split_factor)
        elif pair:
            for copy in panel_copies:
                copy.wait()
            tasks += [solve_panel(first) for first in range(0, x_ref.shape[0], WIDE)]

        def between(b):
            if b == 3 and k == 0:
                for g in range(BLOCK // share, n_row):
                    arrive(g)
            if b >= (1 if k else 3):
                left = BLOCK // 8 - b
                for _ in range(-(-len(tasks) // left)):
                    tasks.pop(0)()

        if k == 0:
            for g in range(BLOCK // share):
                arrive(g)
            source = block(0, 0)
        elif k == 2 * pair:
            source = d_in[...]
        else:
            source = d_ref[...]
        upper, inverse = factor_block([source[8 * j : 8 * j + 8, :] for j in range(BLOCK // 8)], between)
        inverse = jnp.concatenate(inverse, 0)
        w_ref[k % 2] = inverse
        l_ref[at(k), at(k)] = jnp.concatenate(upper, 0).T
        if k + 1 < count:
            cross = full_nt(s_ref[k % 2, at(k + 1), :], inverse)
            l_ref[at(k + 1), at(k)] = cross
            value = d_ref[...] - full_nt(cross, cross)
            if k % 2:
                d_out[...] = value
            else:
                d_ref[...] = value
    if last:
        widen(w_ref[0], w_ref[1], l_ref[at(count - 1), at(count - 2)], *final_refs)
    else:
        s_out[...] = s_ref[1]
        w_out[0][...] = w_ref[0]
        w_out[1][...] = w_ref[1]


def cholesky_pair(pair, n, n_row, where, state, panels):
    anywhere = pl.BlockSpec(memory_space=pl.ANY)
    last = pair * WIDE + WIDE == n
    small = jax.ShapeDtypeStruct((BLOCK, BLOCK), F32)
    square = jax.ShapeDtypeStruct((WIDE, WIDE), BF16)
    shapes, out_specs = [], []
    if not pair:
        window = state[1].shape[1]
        shapes.append(jax.ShapeDtypeStruct((n_row, n // n_row, window), F32))
        out_specs.append(own_vmem())
    shapes.append(jax.ShapeDtypeStruct((n, n), F32))
    out_specs.append(own_vmem())
    slots, rows, _ = panels[0].shape
    total = len(panels) * slots * rows
    solved = []
    if pair:
        solved = [jax.ShapeDtypeStruct((total, n), F32)] + [jax.ShapeDtypeStruct((total, n), BF16)] * 2
        solved += [jax.ShapeDtypeStruct((n, n), BF16)] * 2
    wide = [square] * (2 * (pair > 0) + 2 * last)
    kept = [] if last else [small, jax.ShapeDtypeStruct((n, BLOCK), F32), small, small]
    shapes += solved + wide + kept
    out_specs += [own_vmem()] * len(solved + wide + kept)
    smem = pl.BlockSpec(memory_space=pltpu.SMEM)
    if not pair:
        inputs, in_specs, aliases = [where, *state], [smem] + [anywhere] * len(state), {}
    elif pair == 1:
        inputs, aliases = [*state, where, *panels], {5: 0}
        in_specs = [own_vmem()] * 6 + [smem] + [anywhere] * len(panels)
    else:
        inputs, in_specs, aliases = state, [own_vmem()] * 11, {5 + i: i for i in range(6)}
    out = pl.pallas_call(
        functools.partial(pair_kernel, pair, n, n_row, len(panels)),
        out_shape=shapes,
        in_specs=in_specs,
        out_specs=out_specs,
        input_output_aliases=aliases,
        scratch_shapes=[
            pltpu.VMEM((2, n, BLOCK), F32),
            pltpu.VMEM((BLOCK, BLOCK), F32),
            pltpu.VMEM((2, BLOCK, BLOCK), F32),
            pltpu.SemaphoreType.DMA((max(n_row, len(panels) * slots),)),
        ],
        compiler_params=pltpu.CompilerParams(vmem_limit_bytes=16 * 2**20),
        cost_estimate=pl.CostEstimate(flops=14_000_000_000, bytes_accessed=4 * n * BLOCK * 4, transcendentals=0),
        name=f"cholesky_{pair}",
    )(*inputs)
    window = state[0] if pair else out[0]
    l, *out = out if pair else out[1:]
    solved, out = out[: len(solved)], out[len(solved) :]
    wide, kept = out[: len(wide)], out[len(wide) :]
    return [window, *kept, l, *solved], wide


def finish_kernel(places, n_piece, where_ref, map_ref, g_ref, t_ref, l_ref, x_ref, xh_ref, xl_ref, lh_ref, ll_ref, *refs):
    slots, _, tile, _ = t_ref.shape
    total, n = x_ref.shape
    wide = n // WIDE
    wh_ref, wl_ref = refs[:wide], refs[wide : 2 * wide]
    out_ref, own_ref, diag_ref, p_ref, ch_ref, cl_ref, yh_ref, yl_ref, y_ref, mh_ref, ml_ref = refs[2 * wide :]
    row, col = where_ref[0], where_ref[1]
    chunk = g_ref.shape[1]
    rows = tile // n_piece
    many = slots * rows
    end = n - WIDE
    mh_ref[...], ml_ref[...] = halves(l_ref[end:, :end])
    for i, at in enumerate(places(row, col)):
        p_ref[i * chunk : i * chunk + chunk, :] = g_ref[at]

    def column(k):
        lo, hi = k * WIDE, k * WIDE + WIDE
        rest = p_ref[:, lo:hi]
        if k:
            factor = (mh_ref[...], ml_ref[...]) if lo == end else (lh_ref[lo:hi, :lo], ll_ref[lo:hi, :lo])
            rest = rest - split_nt(ch_ref[:, :lo], cl_ref[:, :lo], *factor)
        x = split_nt(*halves(rest), wh_ref[k][...], wl_ref[k][...])
        ch_ref[:, lo:hi], cl_ref[:, lo:hi] = halves(x)

    def panel(first):
        those = slice(first, first + WIDE)
        rest = x_ref[those, end:] - split_nt(xh_ref[those, :end], xl_ref[those, :end], mh_ref[...], ml_ref[...])
        x = split_nt(*halves(rest), wh_ref[wide - 1][...], wl_ref[wide - 1][...])
        y_ref[those, :] = x
        yh_ref[those, :], yl_ref[those, :] = halves(x)

    def product(i, lo, hi):
        those = slice(i * many, i * many + many)
        if lo == end:
            high, low = yh_ref[those, :], yl_ref[those, :]
        else:
            high, low = xh_ref[those, lo:hi], xl_ref[those, lo:hi]
        value = split_nt(high, low, ch_ref[:, lo:hi], cl_ref[:, lo:hi])
        for s in range(slots):
            at = slice(i * rows, i * rows + rows)
            live = map_ref[row * slots + s] >= col
            old = t_ref[s, 0, at, :] if lo == 0 else out_ref[s, 0, at, :]
            new = old - value[s * rows : (s + 1) * rows]
            out_ref[s, 0, at, :] = jnp.where(live, new, jnp.zeros_like(new))

    batches = list(range(0, total, WIDE))
    column(0)
    column(1)
    for first in batches:
        panel(first)
    column(2)
    for i in range(n_piece):
        product(i, 0, n // 2)
    column(3)
    for i in range(n_piece):
        product(i, n // 2, end)
        product(i, end, n)
    share = diag_ref.shape[0]
    mine = l_ref[pl.ds(pl.multiple_of(row * share, share), share), :]
    block = lax.broadcasted_iota(jnp.int32, mine.shape, 1) // BLOCK
    diag_ref[...] = jnp.where(block <= row * share // BLOCK, mine, jnp.zeros_like(mine))
    mine = pl.ds(pl.multiple_of(col * many, many), many)
    own_ref[:, :, :end] = x_ref[mine, :end].reshape(slots, rows, end)
    own_ref[:, :, end:] = y_ref[mine, :].reshape(slots, rows, WIDE)


def finish(where, tile_map, n_row, panels, gathered, places, trailing, solved, wh, wl):
    tile = trailing.shape[2]
    slots, rows, n = panels[0].shape
    total = len(panels) * slots * rows
    smem = pl.BlockSpec(memory_space=pltpu.SMEM)
    return pl.pallas_call(
        functools.partial(finish_kernel, places, len(panels)),
        out_shape=(
            jax.ShapeDtypeStruct(trailing.shape, F32),
            jax.ShapeDtypeStruct((slots, rows, n), F32),
            jax.ShapeDtypeStruct((n // n_row, n), F32),
        ),
        in_specs=[smem] * 2 + [own_vmem()] * (2 + len(solved) + len(wh) + len(wl)),
        out_specs=[own_vmem()] * 3,
        scratch_shapes=[
            pltpu.VMEM((tile, n), F32),
            pltpu.VMEM((tile, n), BF16),
            pltpu.VMEM((tile, n), BF16),
            pltpu.VMEM((total, WIDE), BF16),
            pltpu.VMEM((total, WIDE), BF16),
            pltpu.VMEM((total, WIDE), F32),
            pltpu.VMEM((WIDE, n - WIDE), BF16),
            pltpu.VMEM((WIDE, n - WIDE), BF16),
        ],
        compiler_params=pltpu.CompilerParams(vmem_limit_bytes=20 * 2**20),
        cost_estimate=pl.CostEstimate(flops=14_000_000_000, bytes_accessed=20 * n * n, transcendentals=0),
        name="finish",
    )(where, tile_map, gathered, trailing, *solved, *wh, *wl)


def choose_kernel(n_col, where_ref, map_ref, *refs):
    count = len(refs) - n_col.bit_length()
    holds, outs = refs[:count], refs[count:]
    row, col = where_ref[0], where_ref[1]
    slots = holds[0].shape[0]
    for m, out in enumerate(outs):
        first = 1 << (m - 1) if m else 0
        for i in range(out.shape[0]):
            total = None
            for e, hold in enumerate(holds):
                for t in range(slots):
                    there = map_ref[(row ^ e) * slots + t] == col ^ (first + i)
                    part = hold[t]
                    total = jnp.where(there, part, jnp.zeros_like(part) if total is None else total)
            out[i] = total


def choose(where, tile_map, holds, n_col):
    _, length, n = holds[0].shape
    smem = pl.BlockSpec(memory_space=pltpu.SMEM)
    sizes = [1] + [1 << m for m in range(n_col.bit_length() - 1)]
    return pl.pallas_call(
        functools.partial(choose_kernel, n_col),
        out_shape=[jax.ShapeDtypeStruct((size, length, n), F32) for size in sizes],
        in_specs=[smem] * 2 + [own_vmem()] * len(holds),
        out_specs=[own_vmem()] * len(sizes),
        compiler_params=pltpu.CompilerParams(vmem_limit_bytes=8 * 2**20),
        name="choose",
    )(where, tile_map, *holds)


def part_kernel(places, bit, where_ref, *refs):
    tiles, (sent_ref, kept_ref) = refs[:-2], refs[-2:]
    length = sent_ref.shape[1]
    upper = (where_ref[0] >> bit) & 1
    for j, place in enumerate(places):
        sent_ref[j] = tiles[j][place, pl.ds(pl.multiple_of((1 - upper) * length, length), length), :]
        kept_ref[j] = tiles[j][place, pl.ds(pl.multiple_of(upper * length, length), length), :]


def part(where, tiles, places, bit):
    _, length, n = tiles[0].shape
    shape = jax.ShapeDtypeStruct((len(tiles), length // 2, n), F32)
    return pl.pallas_call(
        functools.partial(part_kernel, places, bit),
        out_shape=[shape, shape],
        in_specs=[pl.BlockSpec(memory_space=pltpu.SMEM)] + [own_vmem()] * len(tiles),
        out_specs=[own_vmem()] * 2,
        compiler_params=pltpu.CompilerParams(vmem_limit_bytes=8 * 2**20),
        name="part",
    )(where, *tiles)


def flip(x, axis, size, bit):
    return lax.ppermute(x, axis, [(i, i ^ bit) for i in range(size)])


def grow(x, axis, size, bit):
    return jnp.concatenate([x, flip(x, axis, size, bit)], 0)


def fan_out(found, bits, size):
    out = dict(found)
    for bit in bits:
        for p in found:
            out[p | bit] = flip(found[p], "row", size, bit)
    return out


def bits_of(size):
    return [size >> i for i in range(1, size.bit_length())]


def in_order(first, then):
    return lax.optimization_barrier((first, then))


def per_device(n_row, n_col, trailing, panel_block, diag_block, tile_map):
    slots, rows, n = panel_block.shape
    tile = rows * n_col
    row, col = lax.axis_index("row"), lax.axis_index("col")
    core = col & 1
    where = jnp.stack([row, col, core]).astype(jnp.int32)
    row_bits, col_bits = bits_of(n_row), bits_of(n_col)
    half = n // n_row // 2
    width = (n_row // 2 + 1) * BLOCK if packed(n, n_row) else n
    side = lax.dynamic_slice_in_dim(diag_block, core * half, half, 0)
    if packed(n, n_row):
        side = lax.dynamic_slice_in_dim(jnp.concatenate([side, side], 1), row * BLOCK, width, 1)

    early = next(k for k in range(1, len(row_bits) + 1) if slots << k > n_col)
    length = rows >> early
    me = flipped_place(row, n_row) >> (len(row_bits) - early)
    hold = {0: {i: lax.dynamic_slice_in_dim(panel_block, (i ^ me) * length, length, 1) for i in range(1 << early)}}

    def spread_bit(k):
        half_count = 1 << (early - 1 - k)
        for e in list(hold):
            for i in reversed(range(half_count, 2 * half_count)):
                got = flip(hold[e].pop(i), "row", n_row, 1 << k)
                hold.setdefault(e | 1 << k, {})[i - half_count] = got

    mine = {0: side}
    for bit in row_bits:
        mine[bit] = flip(side, "row", n_row, bit)
    first, last = 1 << early - 1, (1 << early) - 1
    later = [i for i in range(first, last)] or [last]
    some = lax.optimization_barrier((*[hold[0][i] for i in later], *[mine[p] for p in row_bits]))
    hold[0].update(zip(later, some))
    mine.update(zip(row_bits, some[len(later) :]))
    for bit in row_bits:
        for p in [p for p in mine if p and p & (2 * bit - 1) == 0]:
            mine[p | bit] = flip(mine[p], "row", n_row, bit)
    found = {0: panel_block, col_bits[0]: flip(panel_block, "col", n_col, col_bits[0])}
    for k in range(early):
        spread_bit(k)
    for bit in col_bits[1:]:
        for p in list(found):
            found[p | bit] = flip(found[p], "col", n_col, bit)
    panels = [found[p] for p in range(n_col)]
    groups = choose(where, tile_map, [hold[e][0] for e in range(1 << early)], n_col)
    tiles = {0: (groups[0], 0)}
    for m in reversed(range(len(col_bits))):
        bit = 1 << m
        for j in list(tiles):
            if j == 0:
                tiles[bit] = (flip(groups[1 + m], "col", n_col, bit), 0)
            elif bit == 1:
                tiles[j | bit] = (flip(tiles[j][0], "col", n_col, bit), 1)
            else:
                tiles[j | bit] = (flip(tiles[j][0][bit:], "col", n_col, bit), 0)
    diag = [diag_block]
    for p in range(1, n_row):
        diag += [mine[p], flip(mine[p], "col", n_col, 1)]
    column = [tiles[j][0] for j in range(n_col)]
    *diag, column[-1] = lax.optimization_barrier((*diag, column[-1]))
    for k in range(early, len(row_bits)):
        length //= 2
        upper = (row >> k) & 1
        if k == early and length % 8 == 0:
            sent, kept = part(where, column, [tiles[j][1] for j in range(n_col)], k)
        else:
            if k == early:
                column = jnp.stack([x[tiles[j][1]] for j, x in enumerate(column)])
            sent = lax.dynamic_slice_in_dim(column, (1 - upper) * length, length, 1)
            kept = lax.dynamic_slice_in_dim(column, upper * length, length, 1)
        column = kept + flip(sent, "row", n_row, 1 << k)

    state, wide = diag, []
    together = {0: column}
    for k in range(n // WIDE):
        state, more = cholesky_pair(k, n, n_row, where, state, panels)
        wide += more
        if k + 1 < n // WIDE:
            at_hand = list(together)
            *state, = lax.optimization_barrier((*state, *[together[p] for p in at_hand]))
            together.update(zip(at_hand, state[-len(at_hand) :]))
            del state[-len(at_hand) :]
            hops = [k + 1] if k + 2 < n // WIDE else list(range(k + 1, len(row_bits) + 1))
            for hop in hops:
                for bit in row_bits:
                    for p in at_hand if hop == hops[0] else list(together):
                        if p & (2 * bit - 1) == 0 and bin(p).count("1") + 1 == hop:
                            together[p | bit] = flip(together[p], "row", n_row, bit)
    wh, wl = wide[::2], wide[1::2]
    column = jnp.stack([together[flipped_place(p, n_row)] for p in range(n_row)])

    chunk = rows // n_row
    if chunk % 8 == 0:
        column = column.reshape(n_row * n_col, chunk, n)

        def places(at_row, at_col):
            here = flipped_place(at_row, n_row)
            return [(q ^ here) * n_col + (j ^ at_col) for j in range(n_col) for q in range(n_row)]
    else:
        order = jnp.arange(n_row, dtype=jnp.int32) ^ flipped_place(row, n_row)
        swapped = jnp.arange(n_col, dtype=jnp.int32) ^ col
        column = column[order][:, swapped].transpose(1, 0, 2, 3).reshape(tile // 8, 8, n)

        def places(at_row, at_col):
            return list(range(tile // 8))

    updated, panel_factor, diag_factor = finish(
        where, tile_map, n_row, panels, column, places, trailing, state[1:], wh, wl
    )
    return updated, panel_factor, diag_factor


def solution(mesh):
    n_row, n_col = mesh.shape["row"], mesh.shape["col"]
    in_specs = (P("row", "col", None, None), P("row", "col", None), P("row", None), P())
    out_specs = (P("row", "col", None, None), P("row", "col", None), P("row", None))
    return jax.shard_map(
        functools.partial(per_device, n_row, n_col),
        mesh=mesh,
        in_specs=in_specs,
        out_specs=out_specs,
        check_vma=False,
    )
```

```python
import functools

import jax
import jax.numpy as jnp
from jax import lax
from jax.experimental import pallas as pl
from jax.experimental.pallas import tpu as pltpu
from jax.sharding import PartitionSpec as P

BLOCK = 128
WIDE = 256
F32, BF16 = jnp.float32, jnp.bfloat16


def spread_row(x, m):
    return jnp.broadcast_to(x[m : m + 1, :], x.shape)


def spread_lane(x, j):
    return jnp.broadcast_to(x[:, j : j + 1], x.shape)


def factor_block(rows_in, between):
    count = len(rows_in)
    work = list(rows_in)
    lane = lax.broadcasted_iota(jnp.int32, (8, BLOCK), 1)
    sub = lax.broadcasted_iota(jnp.int32, (8, BLOCK), 0)
    upper, inverse = [], []
    for b in range(count):
        between(b)
        o = 8 * b
        rows = [spread_row(work[b], m) for m in range(8)]
        p = {(m, l): spread_lane(rows[m], o + l) for m in range(8) for l in range(m + 1)}
        r = list(rows)
        t = [jnp.where(lane == o + m, 1.0, jnp.where(lane >= o, 0.0, rows[m])) for m in range(8)]
        inside = (lane >= o) & (lane < o + 8)
        following = None
        if b + 1 < count:
            c = [spread_lane(work[b + 1], o + m) for m in range(8)]
            following = jnp.where(inside, 0.0, work[b + 1])
        f, ri = {}, []
        for j in range(8):
            ri.append(pl.reciprocal(p[j, j], approx=True))
            for m in range(j + 1, 8):
                f[m, j] = p[m, j] * ri[j]
                for l in range(j + 1, m + 1):
                    if m == j + 1:
                        p[m, l] = p[m, l] - (p[m, j] * p[l, j]) * ri[j]
                    else:
                        p[m, l] = p[m, l] - f[m, j] * p[l, j]
                r[m] = r[m] - f[m, j] * r[j]
                t[m] = t[m] - f[m, j] * t[j]
            if following is not None:
                following = following - c[j] * (jnp.where(lane < o + 8, t[j], r[j]) * ri[j])
                for m in range(j + 1, 8):
                    c[m] = c[m] - c[j] * f[m, j]
        up, inv = None, None
        for m in range(8):
            s = lax.rsqrt(p[m, m])
            um, im = r[m] * s, t[m] * s
            up = um if m == 0 else jnp.where(sub == m, um, up)
            inv = im if m == 0 else jnp.where(sub == m, im, inv)
        upper.append(jnp.where(lane >= sub + o, up, 0.0))
        inverse.append(inv)
        if following is not None:
            work[b + 1] = following
        if b + 2 < count:
            z = [None] * 8
            for m in range(7, -1, -1):
                v = jnp.where(lane < o + 8, t[m], r[m]) * ri[m]
                for l in range(7, m, -1):
                    v = v - f[l, m] * z[l]
                z[m] = v
            for i in range(b + 2, count):
                v = jnp.where(inside, 0.0, work[i])
                for m in range(8):
                    v = v - spread_lane(work[i], o + m) * z[m]
                work[i] = v
    return upper, inverse


def dot_nt(a, b, precision=None):
    return lax.dot_general(a, b, (((1,), (1,)), ((), ())), precision=precision, preferred_element_type=F32)


def full_nt(a, b):
    return dot_nt(a, b, lax.Precision.HIGHEST)


def halves(x):
    high = x.astype(BF16)
    return high, (x - high.astype(F32)).astype(BF16)


def split_nt(ah, al, bh, bl):
    return dot_nt(ah, bh) + (dot_nt(ah, bl) + dot_nt(al, bh))


def flipped_place(index, count):
    place, bit = 0, 1
    while bit < count:
        place = place * 2 + (index & 1)
        index = index >> 1
        bit *= 2
    return place


def packed(n, n_row):
    return n_row * BLOCK == n


def window_block(row, d, n, n_row):
    return (row + d) % n_row if packed(n, n_row) else d


def own_vmem():
    return pl.BlockSpec(memory_space=pltpu.VMEM)


def pair_kernel(pair, n, n_row, n_piece, *refs):
    count, last = n // BLOCK, pair * WIDE + WIDE == n
    start, end = 2 * pair * BLOCK, 2 * pair * BLOCK + WIDE
    refs = list(refs)

    def take(number):
        taken = refs[:number]
        del refs[:number]
        return taken

    if pair:
        win_ref, d_in, s_in, w0_in, w1_in, _ = take(6)
        if pair == 1:
            (where_ref,) = take(1)
            panels = take(n_piece)
        else:
            take(5)
    else:
        (where_ref,) = take(1)
        diag_ref = take(1)[0]
        pieces = take(2 * n_row - 2)
        (win_ref,) = take(1)
    (l_ref,) = take(1)
    if pair:
        x_ref, xh_ref, xl_ref, lh_ref, ll_ref = take(5)
        wide_refs = take(2)
    if last:
        final_refs = take(2)
    else:
        d_out, s_out, *w_out = take(4)
    s_ref, d_ref, w_ref, piece_sem = refs

    def block(i, k):
        if packed(n, n_row):
            if 0 < i - k < n_row // 2:
                return win_ref[k, :, (i - k) * BLOCK : (i - k + 1) * BLOCK].T
            d = (k - i) % n_row
            return win_ref[i, :, d * BLOCK : (d + 1) * BLOCK]
        share = n // n_row
        parts = [win_ref[g, :, k * BLOCK : (k + 1) * BLOCK] for g in range(i * BLOCK // share, (i + 1) * BLOCK // share)]
        return jnp.concatenate(parts, 0)

    def at(i):
        return slice(i * BLOCK, i * BLOCK + BLOCK)

    def rest_of_factor(i, k):
        def work():
            source = s_in[at(i), :] if pair and k < 2 * pair else s_ref[k % 2, at(i), :]
            inverse = w1_in[...] if pair and k < 2 * pair else w_ref[k % 2]
            l_ref[at(i), at(k)] = full_nt(source, inverse)

        return work

    def below(i, k):
        def work():
            value = block(i, k)
            if k:
                value = value - full_nt(l_ref[at(i), : k * BLOCK], l_ref[at(k), : k * BLOCK])
            s_ref[k % 2, at(i), :] = value

        return work

    def next_diagonal(k):
        def work():
            value = block(k, k)
            if k > 1:
                value = value - full_nt(l_ref[at(k), : (k - 1) * BLOCK], l_ref[at(k), : (k - 1) * BLOCK])
            d_ref[...] = value

        return work

    def widen(first, second, cross, high_ref, low_ref):
        mixed = jnp.dot(cross, first, precision=lax.Precision.HIGHEST, preferred_element_type=F32)
        corner = -jnp.dot(second, mixed, precision=lax.Precision.HIGHEST, preferred_element_type=F32)
        whole = jnp.concatenate(
            [jnp.concatenate([first, jnp.zeros_like(first)], 1), jnp.concatenate([corner, second], 1)], 0
        )
        high_ref[...], low_ref[...] = halves(whole)

    panel_copies = []
    if pair == 1:
        slots, rows, _ = panels[0].shape
        for i, panel in enumerate(panels):
            for t in range(slots):
                first = pl.multiple_of(((where_ref[1] ^ i) * slots + t) * rows, rows)
                target = x_ref.at[pl.ds(first, rows), :]
                panel_copies.append(pltpu.make_async_copy(panel.at[t], target, piece_sem.at[i * slots + t]))
        for copy in panel_copies:
            copy.start()

    before = slice(start - WIDE, start)

    def split_factor():
        lh_ref[before, :start], ll_ref[before, :start] = halves(l_ref[before, :start])

    def solve_panel(first):
        def work():
            those = slice(first, first + WIDE)
            rest = x_ref[those, before]
            if pair > 1:
                done = slice(0, start - WIDE)
                rest = rest - split_nt(xh_ref[those, done], xl_ref[those, done], lh_ref[before, done], ll_ref[before, done])
            x = split_nt(*halves(rest), wide_refs[0][...], wide_refs[1][...])
            x_ref[those, before] = x
            xh_ref[those, before], xl_ref[those, before] = halves(x)

        return work

    def split_last():
        lh_ref[start:, :start], ll_ref[start:, :start] = halves(l_ref[start:, :start])

    def reduce_panel(first):
        def work():
            those, done = slice(first, first + WIDE), slice(0, start)
            factor = (lh_ref[start:, done], ll_ref[start:, done])
            x_ref[those, start:] = x_ref[those, start:] - split_nt(xh_ref[those, done], xl_ref[those, done], *factor)

        return work

    if not pair:
        row, core = where_ref[0], where_ref[2]
        share = n // n_row
        half = share // 2
        copies = []
        for d in range(win_ref.shape[2] // BLOCK):
            source = pl.ds(pl.multiple_of(window_block(row, d, n, n_row) * BLOCK, BLOCK), BLOCK)
            target = win_ref.at[row, :, pl.ds(d * BLOCK, BLOCK)]
            copies.append(pltpu.make_async_copy(diag_ref.at[:, source], target, piece_sem.at[row]))
        for i, piece in enumerate(pieces):
            g = row ^ (i // 2 + 1)
            target = win_ref.at[g, pl.ds(pl.multiple_of((core ^ (i % 2)) * half, half), half), :]
            copies.append(pltpu.make_async_copy(piece, target, piece_sem.at[g]))
        for copy in copies:
            copy.start()

    def arrive(g):
        pltpu.make_async_copy(win_ref.at[g], win_ref.at[g], piece_sem.at[g]).wait()

    for k in range(2 * pair, 2 * pair + 2):
        tasks = []
        for i in range(k + 1, count):
            if k:
                tasks.append(rest_of_factor(i, k - 1))
            tasks.append(below(i, k))
        if k + 1 < count:
            tasks.append(next_diagonal(k + 1))
        if pair and k == 2 * pair:
            tasks.append(lambda: widen(w0_in[...], w1_in[...], l_ref[at(k - 1), at(k - 2)], *wide_refs))
            tasks.append(split_factor)
        elif pair:
            for copy in panel_copies:
                copy.wait()
            batches = range(0, x_ref.shape[0], WIDE)
            tasks += [solve_panel(first) for first in batches]
            if last:
                tasks.append(split_last)
                tasks += [reduce_panel(first) for first in batches]

        def between(b):
            if b == 7 and k == 0:
                for g in range(BLOCK // share, n_row):
                    arrive(g)
            if b >= (1 if k else 7):
                left = BLOCK // 8 - b
                for _ in range(-(-len(tasks) // left)):
                    tasks.pop(0)()

        if k == 0:
            for g in range(BLOCK // share):
                arrive(g)
            source = block(0, 0)
        elif k == 2 * pair:
            source = d_in[...]
        else:
            source = d_ref[...]
        upper, inverse = factor_block([source[8 * j : 8 * j + 8, :] for j in range(BLOCK // 8)], between)
        inverse = jnp.concatenate(inverse, 0)
        w_ref[k % 2] = inverse
        l_ref[at(k), at(k)] = jnp.concatenate(upper, 0).T
        if k + 1 < count:
            cross = full_nt(s_ref[k % 2, at(k + 1), :], inverse)
            l_ref[at(k + 1), at(k)] = cross
            value = d_ref[...] - full_nt(cross, cross)
            if k % 2:
                d_out[...] = value
            else:
                d_ref[...] = value
    if last:
        widen(w_ref[0], w_ref[1], l_ref[at(count - 1), at(count - 2)], *final_refs)
    else:
        s_out[...] = s_ref[1]
        w_out[0][...] = w_ref[0]
        w_out[1][...] = w_ref[1]


def cholesky_pair(pair, n, n_row, where, state, panels):
    anywhere = pl.BlockSpec(memory_space=pl.ANY)
    last = pair * WIDE + WIDE == n
    small = jax.ShapeDtypeStruct((BLOCK, BLOCK), F32)
    square = jax.ShapeDtypeStruct((WIDE, WIDE), BF16)
    shapes, out_specs = [], []
    if not pair:
        window = state[1].shape[1]
        shapes.append(jax.ShapeDtypeStruct((n_row, n // n_row, window), F32))
        out_specs.append(own_vmem())
    shapes.append(jax.ShapeDtypeStruct((n, n), F32))
    out_specs.append(own_vmem())
    slots, rows, _ = panels[0].shape
    total = len(panels) * slots * rows
    solved = []
    if pair:
        solved = [jax.ShapeDtypeStruct((total, n), F32)] + [jax.ShapeDtypeStruct((total, n), BF16)] * 2
        solved += [jax.ShapeDtypeStruct((n, n), BF16)] * 2
    wide = [square] * (2 * (pair > 0) + 2 * last)
    kept = [] if last else [small, jax.ShapeDtypeStruct((n, BLOCK), F32), small, small]
    shapes += solved + wide + kept
    out_specs += [own_vmem()] * len(solved + wide + kept)
    smem = pl.BlockSpec(memory_space=pltpu.SMEM)
    if not pair:
        inputs, in_specs, aliases = [where, *state], [smem] + [anywhere] * len(state), {}
    elif pair == 1:
        inputs, aliases = [*state, where, *panels], {5: 0}
        in_specs = [own_vmem()] * 6 + [smem] + [anywhere] * len(panels)
    else:
        inputs, in_specs, aliases = state, [own_vmem()] * 11, {5 + i: i for i in range(6)}
    out = pl.pallas_call(
        functools.partial(pair_kernel, pair, n, n_row, len(panels)),
        out_shape=shapes,
        in_specs=in_specs,
        out_specs=out_specs,
        input_output_aliases=aliases,
        scratch_shapes=[
            pltpu.VMEM((2, n, BLOCK), F32),
            pltpu.VMEM((BLOCK, BLOCK), F32),
            pltpu.VMEM((2, BLOCK, BLOCK), F32),
            pltpu.SemaphoreType.DMA((max(n_row, len(panels) * slots),)),
        ],
        compiler_params=pltpu.CompilerParams(vmem_limit_bytes=16 * 2**20),
        cost_estimate=pl.CostEstimate(flops=14_000_000_000, bytes_accessed=4 * n * BLOCK * 4, transcendentals=0),
        name=f"cholesky_{pair}",
    )(*inputs)
    window = state[0] if pair else out[0]
    l, *out = out if pair else out[1:]
    solved, out = out[: len(solved)], out[len(solved) :]
    wide, kept = out[: len(wide)], out[len(wide) :]
    return [window, *kept, l, *solved], wide


def finish_kernel(places, n_piece, where_ref, map_ref, g_ref, t_ref, l_ref, x_ref, xh_ref, xl_ref, lh_ref, ll_ref, *refs):
    slots, _, tile, _ = t_ref.shape
    total, n = x_ref.shape
    wide = n // WIDE
    wh_ref, wl_ref = refs[:wide], refs[wide : 2 * wide]
    out_hbm, own_hbm, diag_hbm, out_ref, diag_ref, p_ref, ch_ref, cl_ref, yh_ref, yl_ref, y_ref, sem = refs[2 * wide :]
    row, col = where_ref[0], where_ref[1]
    chunk = g_ref.shape[1]
    rows = tile // n_piece
    many = slots * rows
    end = n - WIDE
    share = diag_ref.shape[0]
    copies = []

    def send(source, target):
        copies.append(pltpu.make_async_copy(source, target, sem.at[len(copies)]))
        copies[-1].start()

    for t in range(slots):
        part_rows = pl.ds(pl.multiple_of(col * many + t * rows, rows), rows)
        send(x_ref.at[part_rows, pl.ds(0, end)], own_hbm.at[t, :, pl.ds(0, end)])
    part_rows = l_ref[pl.ds(pl.multiple_of(row * share, share), share), :]
    block = lax.broadcasted_iota(jnp.int32, part_rows.shape, 1) // BLOCK
    diag_ref[...] = jnp.where(block <= row * share // BLOCK, part_rows, jnp.zeros_like(part_rows))
    send(diag_ref, diag_hbm)
    for i, at in enumerate(places(row, col)):
        p_ref[i * chunk : i * chunk + chunk, :] = g_ref[at]

    def column(k):
        lo, hi = k * WIDE, k * WIDE + WIDE
        rest = p_ref[:, lo:hi]
        if k:
            rest = rest - split_nt(ch_ref[:, :lo], cl_ref[:, :lo], lh_ref[lo:hi, :lo], ll_ref[lo:hi, :lo])
        x = split_nt(*halves(rest), wh_ref[k][...], wl_ref[k][...])
        ch_ref[:, lo:hi], cl_ref[:, lo:hi] = halves(x)

    def panel(first):
        those = slice(first, first + WIDE)
        x = split_nt(*halves(x_ref[those, end:]), wh_ref[wide - 1][...], wl_ref[wide - 1][...])
        y_ref[those, :] = x
        yh_ref[those, :], yl_ref[those, :] = halves(x)

    def product(i, lo, hi):
        those = slice(i * many, i * many + many)
        if lo == end:
            high, low = yh_ref[those, :], yl_ref[those, :]
        else:
            high, low = xh_ref[those, lo:hi], xl_ref[those, lo:hi]
        value = split_nt(high, low, ch_ref[:, lo:hi], cl_ref[:, lo:hi])
        for s in range(slots):
            at = slice(i * rows, i * rows + rows)
            live = map_ref[row * slots + s] >= col
            old = t_ref[s, 0, at, :] if lo == 0 else out_ref[s, 0, at, :]
            new = old - value[s * rows : (s + 1) * rows]
            out_ref[s, 0, at, :] = jnp.where(live, new, jnp.zeros_like(new))

    column(0)
    for first in range(0, total, WIDE):
        panel(first)
    for t in range(slots):
        part_rows = pl.ds(pl.multiple_of(col * many + t * rows, rows), rows)
        send(y_ref.at[part_rows, :], own_hbm.at[t, :, pl.ds(end, WIDE)])
    column(1)
    column(2)
    for i in range(n_piece):
        product(i, 0, n // 2)
    column(3)
    for i in range(n_piece):
        product(i, n // 2, end)
        product(i, end, n)
        for t in range(slots):
            region = (t, 0, pl.ds(i * rows, rows), slice(None))
            send(out_ref.at[region], out_hbm.at[region])
    for copy in copies:
        copy.wait()


def finish(where, tile_map, n_row, panels, gathered, places, trailing, solved, wh, wl):
    tile = trailing.shape[2]
    slots, rows, n = panels[0].shape
    total = len(panels) * slots * rows
    smem = pl.BlockSpec(memory_space=pltpu.SMEM)
    return pl.pallas_call(
        functools.partial(finish_kernel, places, len(panels)),
        out_shape=(
            jax.ShapeDtypeStruct(trailing.shape, F32),
            jax.ShapeDtypeStruct((slots, rows, n), F32),
            jax.ShapeDtypeStruct((n // n_row, n), F32),
        ),
        in_specs=[smem] * 2 + [own_vmem()] * (2 + len(solved) + len(wh) + len(wl)),
        out_specs=[pl.BlockSpec(memory_space=pl.ANY)] * 3,
        scratch_shapes=[
            pltpu.VMEM(trailing.shape, F32),
            pltpu.VMEM((n // n_row, n), F32),
            pltpu.VMEM((tile, n), F32),
            pltpu.VMEM((tile, n), BF16),
            pltpu.VMEM((tile, n), BF16),
            pltpu.VMEM((total, WIDE), BF16),
            pltpu.VMEM((total, WIDE), BF16),
            pltpu.VMEM((total, WIDE), F32),
            pltpu.SemaphoreType.DMA((2 * slots + 1 + len(panels) * slots,)),
        ],
        compiler_params=pltpu.CompilerParams(vmem_limit_bytes=20 * 2**20),
        cost_estimate=pl.CostEstimate(flops=14_000_000_000, bytes_accessed=20 * n * n, transcendentals=0),
        name="finish",
    )(where, tile_map, gathered, trailing, *solved, *wh, *wl)


def choose_kernel(n_col, where_ref, map_ref, *refs):
    count = len(refs) - n_col.bit_length()
    holds, outs = refs[:count], refs[count:]
    row, col = where_ref[0], where_ref[1]
    slots = holds[0].shape[0]
    for m, out in enumerate(outs):
        first = 1 << (m - 1) if m else 0
        for i in range(out.shape[0]):
            total = None
            for e, hold in enumerate(holds):
                for t in range(slots):
                    there = map_ref[(row ^ e) * slots + t] == col ^ (first + i)
                    part = hold[t]
                    total = jnp.where(there, part, jnp.zeros_like(part) if total is None else total)
            out[i] = total


def choose(where, tile_map, holds, n_col):
    _, length, n = holds[0].shape
    smem = pl.BlockSpec(memory_space=pltpu.SMEM)
    sizes = [1] + [1 << m for m in range(n_col.bit_length() - 1)]
    return pl.pallas_call(
        functools.partial(choose_kernel, n_col),
        out_shape=[jax.ShapeDtypeStruct((size, length, n), F32) for size in sizes],
        in_specs=[smem] * 2 + [own_vmem()] * len(holds),
        out_specs=[own_vmem()] * len(sizes),
        compiler_params=pltpu.CompilerParams(vmem_limit_bytes=8 * 2**20),
        name="choose",
    )(where, tile_map, *holds)


def part_kernel(places, bit, where_ref, *refs):
    tiles, (sent_ref, kept_ref) = refs[:-2], refs[-2:]
    length = sent_ref.shape[1]
    upper = (where_ref[0] >> bit) & 1
    for j, place in enumerate(places):
        sent_ref[j] = tiles[j][place, pl.ds(pl.multiple_of((1 - upper) * length, length), length), :]
        kept_ref[j] = tiles[j][place, pl.ds(pl.multiple_of(upper * length, length), length), :]


def part(where, tiles, places, bit):
    _, length, n = tiles[0].shape
    shape = jax.ShapeDtypeStruct((len(tiles), length // 2, n), F32)
    return pl.pallas_call(
        functools.partial(part_kernel, places, bit),
        out_shape=[shape, shape],
        in_specs=[pl.BlockSpec(memory_space=pltpu.SMEM)] + [own_vmem()] * len(tiles),
        out_specs=[own_vmem()] * 2,
        compiler_params=pltpu.CompilerParams(vmem_limit_bytes=8 * 2**20),
        name="part",
    )(where, *tiles)


def flip(x, axis, size, bit):
    return lax.ppermute(x, axis, [(i, i ^ bit) for i in range(size)])


def grow(x, axis, size, bit):
    return jnp.concatenate([x, flip(x, axis, size, bit)], 0)


def fan_out(found, bits, size):
    out = dict(found)
    for bit in bits:
        for p in found:
            out[p | bit] = flip(found[p], "row", size, bit)
    return out


def bits_of(size):
    return [size >> i for i in range(1, size.bit_length())]


def in_order(first, then):
    return lax.optimization_barrier((first, then))


def per_device(n_row, n_col, trailing, panel_block, diag_block, tile_map):
    slots, rows, n = panel_block.shape
    tile = rows * n_col
    row, col = lax.axis_index("row"), lax.axis_index("col")
    core = col & 1
    where = jnp.stack([row, col, core]).astype(jnp.int32)
    row_bits, col_bits = bits_of(n_row), bits_of(n_col)
    half = n // n_row // 2
    width = (n_row // 2 + 1) * BLOCK if packed(n, n_row) else n
    side = lax.dynamic_slice_in_dim(diag_block, core * half, half, 0)
    if packed(n, n_row):
        side = lax.dynamic_slice_in_dim(jnp.concatenate([side, side], 1), row * BLOCK, width, 1)

    early = next(k for k in range(1, len(row_bits) + 1) if slots << k > n_col)
    length = rows >> early
    me = flipped_place(row, n_row) >> (len(row_bits) - early)
    hold = {0: {i: lax.dynamic_slice_in_dim(panel_block, (i ^ me) * length, length, 1) for i in range(1 << early)}}

    def spread_bit(k):
        half_count = 1 << (early - 1 - k)
        for e in list(hold):
            for i in reversed(range(half_count, 2 * half_count)):
                got = flip(hold[e].pop(i), "row", n_row, 1 << k)
                hold.setdefault(e | 1 << k, {})[i - half_count] = got

    mine = {0: side}
    for bit in row_bits:
        mine[bit] = flip(side, "row", n_row, bit)
    first, last = 1 << early - 1, (1 << early) - 1
    later = [i for i in range(first, last)] or [last]
    some = lax.optimization_barrier((*[hold[0][i] for i in later], *[mine[p] for p in row_bits]))
    hold[0].update(zip(later, some))
    mine.update(zip(row_bits, some[len(later) :]))
    for bit in row_bits:
        for p in [p for p in mine if p and p & (2 * bit - 1) == 0]:
            mine[p | bit] = flip(mine[p], "row", n_row, bit)
    found = {0: panel_block, col_bits[0]: flip(panel_block, "col", n_col, col_bits[0])}
    for k in range(early):
        spread_bit(k)
    for bit in col_bits[1:]:
        for p in list(found):
            found[p | bit] = flip(found[p], "col", n_col, bit)
    panels = [found[p] for p in range(n_col)]
    groups = choose(where, tile_map, [hold[e][0] for e in range(1 << early)], n_col)
    tiles = {0: (groups[0], 0)}
    for m in reversed(range(len(col_bits))):
        bit = 1 << m
        for j in list(tiles):
            if j == 0:
                tiles[bit] = (flip(groups[1 + m], "col", n_col, bit), 0)
            elif bit == 1:
                tiles[j | bit] = (flip(tiles[j][0], "col", n_col, bit), 1)
            else:
                tiles[j | bit] = (flip(tiles[j][0][bit:], "col", n_col, bit), 0)
    diag = [diag_block]
    for p in range(1, n_row):
        diag += [mine[p], flip(mine[p], "col", n_col, 1)]
    column = [tiles[j][0] for j in range(n_col)]
    *diag, column[-1] = lax.optimization_barrier((*diag, column[-1]))
    for k in range(early, len(row_bits)):
        length //= 2
        upper = (row >> k) & 1
        if k == early and length % 8 == 0:
            sent, kept = part(where, column, [tiles[j][1] for j in range(n_col)], k)
        else:
            if k == early:
                column = jnp.stack([x[tiles[j][1]] for j, x in enumerate(column)])
            sent = lax.dynamic_slice_in_dim(column, (1 - upper) * length, length, 1)
            kept = lax.dynamic_slice_in_dim(column, upper * length, length, 1)
        column = kept + flip(sent, "row", n_row, 1 << k)

    state, wide = diag, []
    together = {0: column}
    for k in range(n // WIDE):
        state, more = cholesky_pair(k, n, n_row, where, state, panels)
        wide += more
        if k + 1 < n // WIDE:
            at_hand = list(together)
            *state, = lax.optimization_barrier((*state, *[together[p] for p in at_hand]))
            together.update(zip(at_hand, state[-len(at_hand) :]))
            del state[-len(at_hand) :]
            hops = [k + 1] if k + 2 < n // WIDE else list(range(k + 1, len(row_bits) + 1))
            for hop in hops:
                for bit in row_bits:
                    for p in at_hand if hop == hops[0] else list(together):
                        if p & (2 * bit - 1) == 0 and bin(p).count("1") + 1 == hop:
                            together[p | bit] = flip(together[p], "row", n_row, bit)
    wh, wl = wide[::2], wide[1::2]
    column = jnp.stack([together[flipped_place(p, n_row)] for p in range(n_row)])

    chunk = rows // n_row
    if chunk % 8 == 0:
        column = column.reshape(n_row * n_col, chunk, n)

        def places(at_row, at_col):
            here = flipped_place(at_row, n_row)
            return [(q ^ here) * n_col + (j ^ at_col) for j in range(n_col) for q in range(n_row)]
    else:
        order = jnp.arange(n_row, dtype=jnp.int32) ^ flipped_place(row, n_row)
        swapped = jnp.arange(n_col, dtype=jnp.int32) ^ col
        column = column[order][:, swapped].transpose(1, 0, 2, 3).reshape(tile // 8, 8, n)

        def places(at_row, at_col):
            return list(range(tile // 8))

    updated, panel_factor, diag_factor = finish(
        where, tile_map, n_row, panels, column, places, trailing, state[1:], wh, wl
    )
    return updated, panel_factor, diag_factor


def solution(mesh):
    n_row, n_col = mesh.shape["row"], mesh.shape["col"]
    in_specs = (P("row", "col", None, None), P("row", "col", None), P("row", None), P())
    out_specs = (P("row", "col", None, None), P("row", "col", None), P("row", None))
    return jax.shard_map(
        functools.partial(per_device, n_row, n_col),
        mesh=mesh,
        in_specs=in_specs,
        out_specs=out_specs,
        check_vma=False,
    )
```

```python
import functools

import jax
import jax.numpy as jnp
from jax import lax
from jax.experimental import pallas as pl
from jax.experimental.pallas import tpu as pltpu
from jax.sharding import PartitionSpec as P

BLOCK = 128
WIDE = 256
F32, BF16 = jnp.float32, jnp.bfloat16


def spread_row(x, m):
    return jnp.broadcast_to(x[m : m + 1, :], x.shape)


def spread_lane(x, j):
    return jnp.broadcast_to(x[:, j : j + 1], x.shape)


def factor_block(rows_in, between):
    count = len(rows_in)
    work = list(rows_in)
    lane = lax.broadcasted_iota(jnp.int32, (8, BLOCK), 1)
    sub = lax.broadcasted_iota(jnp.int32, (8, BLOCK), 0)
    upper, inverse = [], []
    for b in range(count):
        between(b)
        o = 8 * b
        rows = [spread_row(work[b], m) for m in range(8)]
        p = {(m, l): spread_lane(rows[m], o + l) for m in range(8) for l in range(m + 1)}
        r = list(rows)
        t = [jnp.where(lane == o + m, 1.0, jnp.where(lane >= o, 0.0, rows[m])) for m in range(8)]
        inside = (lane >= o) & (lane < o + 8)
        following = None
        if b + 1 < count:
            c = [spread_lane(work[b + 1], o + m) for m in range(8)]
            following = jnp.where(inside, 0.0, work[b + 1])
        f, ri = {}, []
        for j in range(8):
            ri.append(pl.reciprocal(p[j, j], approx=True))
            for m in range(j + 1, 8):
                f[m, j] = p[m, j] * ri[j]
                for l in range(j + 1, m + 1):
                    if m == j + 1:
                        p[m, l] = p[m, l] - (p[m, j] * p[l, j]) * ri[j]
                    else:
                        p[m, l] = p[m, l] - f[m, j] * p[l, j]
                r[m] = r[m] - f[m, j] * r[j]
                t[m] = t[m] - f[m, j] * t[j]
            if following is not None:
                following = following - c[j] * (jnp.where(lane < o + 8, t[j], r[j]) * ri[j])
                for m in range(j + 1, 8):
                    c[m] = c[m] - c[j] * f[m, j]
        up, inv = None, None
        for m in range(8):
            s = lax.rsqrt(p[m, m])
            um, im = r[m] * s, t[m] * s
            up = um if m == 0 else jnp.where(sub == m, um, up)
            inv = im if m == 0 else jnp.where(sub == m, im, inv)
        upper.append(jnp.where(lane >= sub + o, up, 0.0))
        inverse.append(inv)
        if following is not None:
            work[b + 1] = following
        if b + 2 < count:
            z = [None] * 8
            for m in range(7, -1, -1):
                v = jnp.where(lane < o + 8, t[m], r[m]) * ri[m]
                for l in range(7, m, -1):
                    v = v - f[l, m] * z[l]
                z[m] = v
            for i in range(b + 2, count):
                v = jnp.where(inside, 0.0, work[i])
                for m in range(8):
                    v = v - spread_lane(work[i], o + m) * z[m]
                work[i] = v
    return upper, inverse


def dot_nt(a, b, precision=None):
    return lax.dot_general(a, b, (((1,), (1,)), ((), ())), precision=precision, preferred_element_type=F32)


def full_nt(a, b):
    return dot_nt(a, b, lax.Precision.HIGHEST)


def halves(x):
    high = x.astype(BF16)
    return high, (x - high.astype(F32)).astype(BF16)


def split_nt(ah, al, bh, bl):
    return dot_nt(ah, bh) + (dot_nt(ah, bl) + dot_nt(al, bh))


def flipped_place(index, count):
    place, bit = 0, 1
    while bit < count:
        place = place * 2 + (index & 1)
        index = index >> 1
        bit *= 2
    return place


def packed(n, n_row):
    return n_row * BLOCK == n


def window_block(row, d, n, n_row):
    return (row + d) % n_row if packed(n, n_row) else d


def own_vmem():
    return pl.BlockSpec(memory_space=pltpu.VMEM)


def pair_kernel(pair, n, n_row, n_piece, *refs):
    count, last = n // BLOCK, pair * WIDE + WIDE == n
    start, end = 2 * pair * BLOCK, 2 * pair * BLOCK + WIDE
    refs = list(refs)

    def take(number):
        taken = refs[:number]
        del refs[:number]
        return taken

    if pair:
        win_ref, d_in, s_in, w0_in, w1_in, _ = take(6)
        if pair == 1:
            (where_ref,) = take(1)
            panels = take(n_piece)
        else:
            take(5)
    else:
        (where_ref,) = take(1)
        diag_ref = take(1)[0]
        pieces = take(2 * n_row - 2)
        (win_ref,) = take(1)
    (l_ref,) = take(1)
    if pair:
        x_ref, xh_ref, xl_ref, lh_ref, ll_ref = take(5)
        wide_refs = take(2)
    if last:
        final_refs = take(2)
    else:
        d_out, s_out, *w_out = take(4)
    s_ref, d_ref, w_ref, piece_sem = refs

    def block(i, k):
        if packed(n, n_row):
            if 0 < i - k < n_row // 2:
                return win_ref[k, :, (i - k) * BLOCK : (i - k + 1) * BLOCK].T
            d = (k - i) % n_row
            return win_ref[i, :, d * BLOCK : (d + 1) * BLOCK]
        share = n // n_row
        parts = [win_ref[g, :, k * BLOCK : (k + 1) * BLOCK] for g in range(i * BLOCK // share, (i + 1) * BLOCK // share)]
        return jnp.concatenate(parts, 0)

    def at(i):
        return slice(i * BLOCK, i * BLOCK + BLOCK)

    def rest_of_factor(i, k):
        def work():
            source = s_in[at(i), :] if pair and k < 2 * pair else s_ref[k % 2, at(i), :]
            inverse = w1_in[...] if pair and k < 2 * pair else w_ref[k % 2]
            l_ref[at(i), at(k)] = full_nt(source, inverse)

        return work

    def below(i, k):
        def work():
            value = block(i, k)
            if k:
                value = value - full_nt(l_ref[at(i), : k * BLOCK], l_ref[at(k), : k * BLOCK])
            s_ref[k % 2, at(i), :] = value

        return work

    def next_diagonal(k):
        def work():
            value = block(k, k)
            if k > 1:
                value = value - full_nt(l_ref[at(k), : (k - 1) * BLOCK], l_ref[at(k), : (k - 1) * BLOCK])
            d_ref[...] = value

        return work

    def widen(first, second, cross, high_ref, low_ref):
        mixed = jnp.dot(cross, first, precision=lax.Precision.HIGHEST, preferred_element_type=F32)
        corner = -jnp.dot(second, mixed, precision=lax.Precision.HIGHEST, preferred_element_type=F32)
        whole = jnp.concatenate(
            [jnp.concatenate([first, jnp.zeros_like(first)], 1), jnp.concatenate([corner, second], 1)], 0
        )
        high_ref[...], low_ref[...] = halves(whole)

    panel_copies = []
    if pair == 1:
        slots, rows, _ = panels[0].shape
        for i, panel in enumerate(panels):
            for t in range(slots):
                first = pl.multiple_of(((where_ref[1] ^ i) * slots + t) * rows, rows)
                target = x_ref.at[pl.ds(first, rows), :]
                panel_copies.append(pltpu.make_async_copy(panel.at[t], target, piece_sem.at[i * slots + t]))
        for copy in panel_copies:
            copy.start()

    before = slice(start - WIDE, start)

    def split_factor():
        lh_ref[before, :start], ll_ref[before, :start] = halves(l_ref[before, :start])

    def solve_panel(first):
        def work():
            those = slice(first, first + WIDE)
            rest = x_ref[those, before]
            if pair > 1:
                done = slice(0, start - WIDE)
                rest = rest - split_nt(xh_ref[those, done], xl_ref[those, done], lh_ref[before, done], ll_ref[before, done])
            x = split_nt(*halves(rest), wide_refs[0][...], wide_refs[1][...])
            x_ref[those, before] = x
            xh_ref[those, before], xl_ref[those, before] = halves(x)

        return work

    def split_last():
        lh_ref[start:, :start], ll_ref[start:, :start] = halves(l_ref[start:, :start])

    def reduce_panel(first):
        def work():
            those, done = slice(first, first + WIDE), slice(0, start)
            factor = (lh_ref[start:, done], ll_ref[start:, done])
            x_ref[those, start:] = x_ref[those, start:] - split_nt(xh_ref[those, done], xl_ref[those, done], *factor)

        return work

    if not pair:
        row, core = where_ref[0], where_ref[2]
        share = n // n_row
        half = share // 2
        copies = []
        for d in range(win_ref.shape[2] // BLOCK):
            source = pl.ds(pl.multiple_of(window_block(row, d, n, n_row) * BLOCK, BLOCK), BLOCK)
            target = win_ref.at[row, :, pl.ds(d * BLOCK, BLOCK)]
            copies.append(pltpu.make_async_copy(diag_ref.at[:, source], target, piece_sem.at[row]))
        for i, piece in enumerate(pieces):
            g = row ^ (i // 2 + 1)
            target = win_ref.at[g, pl.ds(pl.multiple_of((core ^ (i % 2)) * half, half), half), :]
            copies.append(pltpu.make_async_copy(piece, target, piece_sem.at[g]))
        for copy in copies:
            copy.start()

    def arrive(g):
        pltpu.make_async_copy(win_ref.at[g], win_ref.at[g], piece_sem.at[g]).wait()

    for k in range(2 * pair, 2 * pair + 2):
        tasks = []
        for i in range(k + 1, count):
            if k:
                tasks.append(rest_of_factor(i, k - 1))
            tasks.append(below(i, k))
        if k + 1 < count:
            tasks.append(next_diagonal(k + 1))
        if pair and k == 2 * pair:
            tasks.append(lambda: widen(w0_in[...], w1_in[...], l_ref[at(k - 1), at(k - 2)], *wide_refs))
            tasks.append(split_factor)
        elif pair:
            for copy in panel_copies:
                copy.wait()
            batches = range(0, x_ref.shape[0], WIDE)
            tasks += [solve_panel(first) for first in batches]
            if last:
                tasks.append(split_last)
                tasks += [reduce_panel(first) for first in batches]

        def between(b):
            if b == 7 and k == 0:
                for g in range(BLOCK // share, n_row):
                    arrive(g)
            if b >= (1 if k else 7):
                left = BLOCK // 8 - b
                for _ in range(-(-len(tasks) // left)):
                    tasks.pop(0)()

        if k == 0:
            for g in range(BLOCK // share):
                arrive(g)
            source = block(0, 0)
        elif k == 2 * pair:
            source = d_in[...]
        else:
            source = d_ref[...]
        upper, inverse = factor_block([source[8 * j : 8 * j + 8, :] for j in range(BLOCK // 8)], between)
        inverse = jnp.concatenate(inverse, 0)
        w_ref[k % 2] = inverse
        l_ref[at(k), at(k)] = jnp.concatenate(upper, 0).T
        if k + 1 < count:
            cross = full_nt(s_ref[k % 2, at(k + 1), :], inverse)
            l_ref[at(k + 1), at(k)] = cross
            value = d_ref[...] - full_nt(cross, cross)
            if k % 2:
                d_out[...] = value
            else:
                d_ref[...] = value
    if last:
        widen(w_ref[0], w_ref[1], l_ref[at(count - 1), at(count - 2)], *final_refs)
    else:
        s_out[...] = s_ref[1]
        w_out[0][...] = w_ref[0]
        w_out[1][...] = w_ref[1]


def cholesky_pair(pair, n, n_row, where, state, panels):
    anywhere = pl.BlockSpec(memory_space=pl.ANY)
    last = pair * WIDE + WIDE == n
    small = jax.ShapeDtypeStruct((BLOCK, BLOCK), F32)
    square = jax.ShapeDtypeStruct((WIDE, WIDE), BF16)
    shapes, out_specs = [], []
    if not pair:
        window = state[1].shape[1]
        shapes.append(jax.ShapeDtypeStruct((n_row, n // n_row, window), F32))
        out_specs.append(own_vmem())
    shapes.append(jax.ShapeDtypeStruct((n, n), F32))
    out_specs.append(own_vmem())
    slots, rows, _ = panels[0].shape
    total = len(panels) * slots * rows
    solved = []
    if pair:
        solved = [jax.ShapeDtypeStruct((total, n), F32)] + [jax.ShapeDtypeStruct((total, n), BF16)] * 2
        solved += [jax.ShapeDtypeStruct((n, n), BF16)] * 2
    wide = [square] * (2 * (pair > 0) + 2 * last)
    kept = [] if last else [small, jax.ShapeDtypeStruct((n, BLOCK), F32), small, small]
    shapes += solved + wide + kept
    out_specs += [own_vmem()] * len(solved + wide + kept)
    smem = pl.BlockSpec(memory_space=pltpu.SMEM)
    if not pair:
        inputs, in_specs, aliases = [where, *state], [smem] + [anywhere] * len(state), {}
    elif pair == 1:
        inputs, aliases = [*state, where, *panels], {5: 0}
        in_specs = [own_vmem()] * 6 + [smem] + [anywhere] * len(panels)
    else:
        inputs, in_specs, aliases = state, [own_vmem()] * 11, {5 + i: i for i in range(6)}
    out = pl.pallas_call(
        functools.partial(pair_kernel, pair, n, n_row, len(panels)),
        out_shape=shapes,
        in_specs=in_specs,
        out_specs=out_specs,
        input_output_aliases=aliases,
        scratch_shapes=[
            pltpu.VMEM((2, n, BLOCK), F32),
            pltpu.VMEM((BLOCK, BLOCK), F32),
            pltpu.VMEM((2, BLOCK, BLOCK), F32),
            pltpu.SemaphoreType.DMA((max(n_row, len(panels) * slots),)),
        ],
        compiler_params=pltpu.CompilerParams(vmem_limit_bytes=16 * 2**20),
        cost_estimate=pl.CostEstimate(flops=14_000_000_000, bytes_accessed=4 * n * BLOCK * 4, transcendentals=0),
        name=f"cholesky_{pair}",
    )(*inputs)
    window = state[0] if pair else out[0]
    l, *out = out if pair else out[1:]
    solved, out = out[: len(solved)], out[len(solved) :]
    wide, kept = out[: len(wide)], out[len(wide) :]
    return [window, *kept, l, *solved], wide


def finish_kernel(places, n_piece, where_ref, map_ref, g_ref, t_ref, l_ref, x_ref, xh_ref, xl_ref, lh_ref, ll_ref, *refs):
    slots, _, tile, _ = t_ref.shape
    total, n = x_ref.shape
    wide = n // WIDE
    wh_ref, wl_ref = refs[:wide], refs[wide : 2 * wide]
    out_hbm, own_hbm, diag_hbm, out_ref, diag_ref, p_ref, ch_ref, cl_ref, yh_ref, yl_ref, y_ref, sem = refs[2 * wide :]
    row, col = where_ref[0], where_ref[1]
    chunk = g_ref.shape[1]
    rows = tile // n_piece
    many = slots * rows
    end = n - WIDE
    share = diag_ref.shape[0]
    copies = []

    def send(source, target):
        copies.append(pltpu.make_async_copy(source, target, sem.at[len(copies)]))
        copies[-1].start()

    for t in range(slots):
        part_rows = pl.ds(pl.multiple_of(col * many + t * rows, rows), rows)
        send(x_ref.at[part_rows, pl.ds(0, end)], own_hbm.at[t, :, pl.ds(0, end)])
    part_rows = l_ref[pl.ds(pl.multiple_of(row * share, share), share), :]
    block = lax.broadcasted_iota(jnp.int32, part_rows.shape, 1) // BLOCK
    diag_ref[...] = jnp.where(block <= row * share // BLOCK, part_rows, jnp.zeros_like(part_rows))
    send(diag_ref, diag_hbm)
    for i, at in enumerate(places(row, col)):
        p_ref[i * chunk : i * chunk + chunk, :] = g_ref[at]

    def column(k, first):
        lo, hi = k * WIDE, k * WIDE + WIDE
        those = slice(first, first + WIDE)
        rest = p_ref[those, lo:hi]
        if k:
            rest = rest - split_nt(ch_ref[those, :lo], cl_ref[those, :lo], lh_ref[lo:hi, :lo], ll_ref[lo:hi, :lo])
        x = split_nt(*halves(rest), wh_ref[k][...], wl_ref[k][...])
        ch_ref[those, lo:hi], cl_ref[those, lo:hi] = halves(x)

    def panel(first):
        those = slice(first, first + WIDE)
        x = split_nt(*halves(x_ref[those, end:]), wh_ref[wide - 1][...], wl_ref[wide - 1][...])
        y_ref[those, :] = x
        yh_ref[those, :], yl_ref[those, :] = halves(x)

    def product(i, lo, hi):
        those = slice(i * many, i * many + many)
        high, low = xh_ref[those, lo : min(hi, end)], xl_ref[those, lo : min(hi, end)]
        if hi > end:
            high = jnp.concatenate([high, yh_ref[those, :]], 1)
            low = jnp.concatenate([low, yl_ref[those, :]], 1)
        value = split_nt(high, low, ch_ref[:, lo:hi], cl_ref[:, lo:hi])
        for s in range(slots):
            at = slice(i * rows, i * rows + rows)
            live = map_ref[row * slots + s] >= col
            old = t_ref[s, 0, at, :] if lo == 0 else out_ref[s, 0, at, :]
            new = old - value[s * rows : (s + 1) * rows]
            out_ref[s, 0, at, :] = jnp.where(live, new, jnp.zeros_like(new))

    batches = range(0, tile, WIDE)
    for first in batches:
        column(0, first)
    for first in range(0, total, WIDE):
        panel(first)
    for t in range(slots):
        part_rows = pl.ds(pl.multiple_of(col * many + t * rows, rows), rows)
        send(y_ref.at[part_rows, :], own_hbm.at[t, :, pl.ds(end, WIDE)])
    for first in batches:
        column(1, first)
    solves = [(k, first) for k in range(2, wide) for first in batches]
    for i in range(n_piece):
        for _ in range(-(-len(solves) // (n_piece - i))):
            column(*solves.pop(0))
        product(i, 0, n // 2)
    for i in range(n_piece):
        product(i, n // 2, n)
        for t in range(slots):
            region = (t, 0, pl.ds(i * rows, rows), slice(None))
            send(out_ref.at[region], out_hbm.at[region])
    for copy in copies:
        copy.wait()


def finish(where, tile_map, n_row, panels, gathered, places, trailing, solved, wh, wl):
    tile = trailing.shape[2]
    slots, rows, n = panels[0].shape
    total = len(panels) * slots * rows
    smem = pl.BlockSpec(memory_space=pltpu.SMEM)
    return pl.pallas_call(
        functools.partial(finish_kernel, places, len(panels)),
        out_shape=(
            jax.ShapeDtypeStruct(trailing.shape, F32),
            jax.ShapeDtypeStruct((slots, rows, n), F32),
            jax.ShapeDtypeStruct((n // n_row, n), F32),
        ),
        in_specs=[smem] * 2 + [own_vmem()] * (2 + len(solved) + len(wh) + len(wl)),
        out_specs=[pl.BlockSpec(memory_space=pl.ANY)] * 3,
        scratch_shapes=[
            pltpu.VMEM(trailing.shape, F32),
            pltpu.VMEM((n // n_row, n), F32),
            pltpu.VMEM((tile, n), F32),
            pltpu.VMEM((tile, n), BF16),
            pltpu.VMEM((tile, n), BF16),
            pltpu.VMEM((total, WIDE), BF16),
            pltpu.VMEM((total, WIDE), BF16),
            pltpu.VMEM((total, WIDE), F32),
            pltpu.SemaphoreType.DMA((2 * slots + 1 + len(panels) * slots,)),
        ],
        compiler_params=pltpu.CompilerParams(vmem_limit_bytes=20 * 2**20),
        cost_estimate=pl.CostEstimate(flops=14_000_000_000, bytes_accessed=20 * n * n, transcendentals=0),
        name="finish",
    )(where, tile_map, gathered, trailing, *solved, *wh, *wl)


def choose_kernel(n_col, where_ref, map_ref, *refs):
    count = len(refs) - n_col.bit_length()
    holds, outs = refs[:count], refs[count:]
    row, col = where_ref[0], where_ref[1]
    slots = holds[0].shape[0]
    for m, out in enumerate(outs):
        first = 1 << (m - 1) if m else 0
        for i in range(out.shape[0]):
            total = None
            for e, hold in enumerate(holds):
                for t in range(slots):
                    there = map_ref[(row ^ e) * slots + t] == col ^ (first + i)
                    part = hold[t]
                    total = jnp.where(there, part, jnp.zeros_like(part) if total is None else total)
            out[i] = total


def choose(where, tile_map, holds, n_col):
    _, length, n = holds[0].shape
    smem = pl.BlockSpec(memory_space=pltpu.SMEM)
    sizes = [1] + [1 << m for m in range(n_col.bit_length() - 1)]
    return pl.pallas_call(
        functools.partial(choose_kernel, n_col),
        out_shape=[jax.ShapeDtypeStruct((size, length, n), F32) for size in sizes],
        in_specs=[smem] * 2 + [own_vmem()] * len(holds),
        out_specs=[own_vmem()] * len(sizes),
        compiler_params=pltpu.CompilerParams(vmem_limit_bytes=8 * 2**20),
        name="choose",
    )(where, tile_map, *holds)


def part_kernel(places, bit, where_ref, *refs):
    tiles, (sent_ref, kept_ref) = refs[:-2], refs[-2:]
    length = sent_ref.shape[1]
    upper = (where_ref[0] >> bit) & 1
    for j, place in enumerate(places):
        sent_ref[j] = tiles[j][place, pl.ds(pl.multiple_of((1 - upper) * length, length), length), :]
        kept_ref[j] = tiles[j][place, pl.ds(pl.multiple_of(upper * length, length), length), :]


def part(where, tiles, places, bit):
    _, length, n = tiles[0].shape
    shape = jax.ShapeDtypeStruct((len(tiles), length // 2, n), F32)
    return pl.pallas_call(
        functools.partial(part_kernel, places, bit),
        out_shape=[shape, shape],
        in_specs=[pl.BlockSpec(memory_space=pltpu.SMEM)] + [own_vmem()] * len(tiles),
        out_specs=[own_vmem()] * 2,
        compiler_params=pltpu.CompilerParams(vmem_limit_bytes=8 * 2**20),
        name="part",
    )(where, *tiles)


def flip(x, axis, size, bit):
    return lax.ppermute(x, axis, [(i, i ^ bit) for i in range(size)])


def grow(x, axis, size, bit):
    return jnp.concatenate([x, flip(x, axis, size, bit)], 0)


def fan_out(found, bits, size):
    out = dict(found)
    for bit in bits:
        for p in found:
            out[p | bit] = flip(found[p], "row", size, bit)
    return out


def bits_of(size):
    return [size >> i for i in range(1, size.bit_length())]


def in_order(first, then):
    return lax.optimization_barrier((first, then))


def per_device(n_row, n_col, trailing, panel_block, diag_block, tile_map):
    slots, rows, n = panel_block.shape
    tile = rows * n_col
    row, col = lax.axis_index("row"), lax.axis_index("col")
    core = col & 1
    where = jnp.stack([row, col, core]).astype(jnp.int32)
    row_bits, col_bits = bits_of(n_row), bits_of(n_col)
    half = n // n_row // 2
    width = (n_row // 2 + 1) * BLOCK if packed(n, n_row) else n
    side = lax.dynamic_slice_in_dim(diag_block, core * half, half, 0)
    if packed(n, n_row):
        side = lax.dynamic_slice_in_dim(jnp.concatenate([side, side], 1), row * BLOCK, width, 1)

    early = next(k for k in range(1, len(row_bits) + 1) if slots << k > n_col)
    length = rows >> early
    me = flipped_place(row, n_row) >> (len(row_bits) - early)
    hold = {0: {i: lax.dynamic_slice_in_dim(panel_block, (i ^ me) * length, length, 1) for i in range(1 << early)}}

    def spread_bit(k):
        half_count = 1 << (early - 1 - k)
        for e in list(hold):
            for i in reversed(range(half_count, 2 * half_count)):
                got = flip(hold[e].pop(i), "row", n_row, 1 << k)
                hold.setdefault(e | 1 << k, {})[i - half_count] = got

    mine = {0: side}
    for bit in row_bits:
        mine[bit] = flip(side, "row", n_row, bit)
    first, last = 1 << early - 1, (1 << early) - 1
    later = [i for i in range(first, last)] or [last]
    some = lax.optimization_barrier((*[hold[0][i] for i in later], *[mine[p] for p in row_bits]))
    hold[0].update(zip(later, some))
    mine.update(zip(row_bits, some[len(later) :]))
    for bit in row_bits:
        for p in [p for p in mine if p and p & (2 * bit - 1) == 0]:
            mine[p | bit] = flip(mine[p], "row", n_row, bit)
    found = {0: panel_block, col_bits[0]: flip(panel_block, "col", n_col, col_bits[0])}
    for k in range(early):
        spread_bit(k)
    for bit in col_bits[1:]:
        for p in list(found):
            found[p | bit] = flip(found[p], "col", n_col, bit)
    panels = [found[p] for p in range(n_col)]
    groups = choose(where, tile_map, [hold[e][0] for e in range(1 << early)], n_col)
    tiles = {0: (groups[0], 0)}
    for m in reversed(range(len(col_bits))):
        bit = 1 << m
        for j in list(tiles):
            if j == 0:
                tiles[bit] = (flip(groups[1 + m], "col", n_col, bit), 0)
            elif bit == 1:
                tiles[j | bit] = (flip(tiles[j][0], "col", n_col, bit), 1)
            else:
                tiles[j | bit] = (flip(tiles[j][0][bit:], "col", n_col, bit), 0)
    diag = [diag_block]
    for p in range(1, n_row):
        diag += [mine[p], flip(mine[p], "col", n_col, 1)]
    column = [tiles[j][0] for j in range(n_col)]
    *diag, column[-1] = lax.optimization_barrier((*diag, column[-1]))
    for k in range(early, len(row_bits)):
        length //= 2
        upper = (row >> k) & 1
        if k == early and length % 8 == 0:
            sent, kept = part(where, column, [tiles[j][1] for j in range(n_col)], k)
        else:
            if k == early:
                column = jnp.stack([x[tiles[j][1]] for j, x in enumerate(column)])
            sent = lax.dynamic_slice_in_dim(column, (1 - upper) * length, length, 1)
            kept = lax.dynamic_slice_in_dim(column, upper * length, length, 1)
        column = kept + flip(sent, "row", n_row, 1 << k)

    state, wide = diag, []
    together = {0: column}
    for k in range(n // WIDE):
        state, more = cholesky_pair(k, n, n_row, where, state, panels)
        wide += more
        if k + 1 < n // WIDE:
            at_hand = list(together)
            *state, = lax.optimization_barrier((*state, *[together[p] for p in at_hand]))
            together.update(zip(at_hand, state[-len(at_hand) :]))
            del state[-len(at_hand) :]
            hops = [k + 1] if k + 2 < n // WIDE else list(range(k + 1, len(row_bits) + 1))
            for hop in hops:
                for bit in row_bits:
                    for p in at_hand if hop == hops[0] else list(together):
                        if p & (2 * bit - 1) == 0 and bin(p).count("1") + 1 == hop:
                            together[p | bit] = flip(together[p], "row", n_row, bit)
    wh, wl = wide[::2], wide[1::2]
    column = jnp.stack([together[flipped_place(p, n_row)] for p in range(n_row)])

    chunk = rows // n_row
    if chunk % 8 == 0:
        column = column.reshape(n_row * n_col, chunk, n)

        def places(at_row, at_col):
            here = flipped_place(at_row, n_row)
            return [(q ^ here) * n_col + (j ^ at_col) for j in range(n_col) for q in range(n_row)]
    else:
        order = jnp.arange(n_row, dtype=jnp.int32) ^ flipped_place(row, n_row)
        swapped = jnp.arange(n_col, dtype=jnp.int32) ^ col
        column = column[order][:, swapped].transpose(1, 0, 2, 3).reshape(tile // 8, 8, n)

        def places(at_row, at_col):
            return list(range(tile // 8))

    updated, panel_factor, diag_factor = finish(
        where, tile_map, n_row, panels, column, places, trailing, state[1:], wh, wl
    )
    return updated, panel_factor, diag_factor


def solution(mesh):
    n_row, n_col = mesh.shape["row"], mesh.shape["col"]
    in_specs = (P("row", "col", None, None), P("row", "col", None), P("row", None), P())
    out_specs = (P("row", "col", None, None), P("row", "col", None), P("row", None))
    return jax.shard_map(
        functools.partial(per_device, n_row, n_col),
        mesh=mesh,
        in_specs=in_specs,
        out_specs=out_specs,
        check_vma=False,
    )
```
